512 devices in a mesh: section: 32 (over y, x, core), dp: 16 (over z).
Axes of the slice: x: 4, y: 4, z: 16, core: 2. Of those that a mesh axis runs over, the one named last changes fastest.
Arguments:
- saved: bfloat16 [32, 16, 4, 2, 32, 4096], P('section', 'dp'), may hold values from -6 to 6
- incoming: bfloat16 [32, 16, 2, 32, 4096], P('section', 'dp'), may hold values from -6 to 6
- head: bfloat16 [3, 16, 32, 4096], P(None, 'dp'), may hold values from -6 to 6
- down_weight: bfloat16 [32, 4096, 256], P('section', 'dp'), may hold values from -0.09375 to 0.09375
- up_weight: bfloat16 [32, 4096, 256], P('section', 'dp'), may hold values from -0.1875 to 0.1875
- adopt: int32 [32, 16, 4], replicated, may hold values from -1 to 1, as said below
- live: int32 [16], replicated, may hold values from 0 to 1, as said below
Outputs:
- leaving: bfloat16 [32, 16, 2, 32, 4096], P('section', 'dp')
- grad_up: bfloat16 [32, 4096, 256], P('section', 'dp')
The draws below stay inside these ranges and needn't reach their ends.
Inputs may be any that keep to these rules, and one draw needn't show every extreme that they name: `adopt`: values -1, 0, 1. A device (s, p) has either all 4 entries 0 or all nonzero (it failed); failed devices of one section are 4 or more relays apart on the cycle, so a device adopts at most one micro-batch in a step; every section has a failed device, and some device adopts in every step. `live`: both values occur.
All inputs are finite; a program needn't handle non-finite values.
Results may differ from the reference program's by a relative error of at most 0.019.
Values may be sent and summed in bfloat16 or wider, within the bound.
A program may use at most 64 MiB of HBM per device.

```python
import math
import jax
import jax.numpy as jnp
from jax import lax

D = 4096
R = 256
TOK = 32
K = 4
SECTIONS = 32
PIPES = 16


def draw_adopt(key, part):
    key = jax.random.fold_in(key, 11)
    first_key, second_key, third_key = jax.random.split(key, 3)
    offsets = jax.random.randint(first_key, (SECTIONS, 1), 0, 4)
    pipe_index = jnp.arange(PIPES)[None, :]
    spaced = (pipe_index - offsets) % 4 == 0
    coin_flips = jax.random.randint(second_key, (SECTIONS, PIPES), 0, 2)
    failed = spaced & ((coin_flips == 1) | (pipe_index == offsets))
    direction = jax.random.randint(third_key, (SECTIONS, PIPES, K), 0, 2) * 2 - 1
    return jnp.where(failed[:, :, None], direction, 0).astype(jnp.int32)


def draw_live(key, part):
    key = jax.random.fold_in(key, 23)
    first_key, second_key, third_key = jax.random.split(key, 3)
    coin_flips = jax.random.randint(first_key, (PIPES,), 0, 2)
    dead_pipe = jax.random.randint(second_key, (), 0, PIPES)
    alive_pipe = (dead_pipe + 1 + jax.random.randint(third_key, (), 0, PIPES - 1)) % PIPES
    positions = jnp.arange(PIPES)
    coin_flips = jnp.where(positions == dead_pipe, 0, jnp.where(positions == alive_pipe, 1, coin_flips))
    return coin_flips.astype(jnp.int32)


def level_of(key, dims, pieces, least, largest):
    loudness, own = 1.0, jax.random.fold_in(key, 6)
    for dim, shards_of in pieces:
        steps = jnp.exp(jax.random.uniform(jax.random.fold_in(own, dim), (shards_of,), jnp.float32, least / len(pieces), largest / len(pieces)))
        loudness = loudness * jnp.repeat(steps, dims[dim] // shards_of).reshape([-1 if axis == dim else 1 for axis in range(len(dims))])
    return loudness


def bell_draw(own_key, dims, spread, reach, cuts=(), kind=jnp.bfloat16):
    values = jax.random.normal(own_key, dims, jnp.float32) * spread
    if len(cuts) > 0:
        values = level_of(own_key, dims, cuts, -0.22, 0.18) * values
    return jnp.clip(values, min=-reach, max=reach).astype(kind)


def setup_inputs(seed: int = 0) -> dict:
    key_list = jax.random.split(jax.random.key(seed), 8)
    return {
        "saved": bell_draw(key_list[0], (SECTIONS, PIPES, K, 2, TOK, D), 1.0, 6.0, ((0, 32), (1, 16))),
        "incoming": bell_draw(key_list[1], (SECTIONS, PIPES, 2, TOK, D), 1.0, 6.0, ((0, 32), (1, 16))),
        "head": bell_draw(key_list[2], (K - 1, PIPES, TOK, D), 1.0, 6.0, ((1, 16),)),
        "down_weight": bell_draw(key_list[3], (SECTIONS, D, R), D ** -0.5, 0.09375, ((0, 32), (1, 16))),
        "up_weight": bell_draw(key_list[4], (SECTIONS, D, R), (4 * R) ** -0.5, 0.1875, ((0, 32), (1, 16))),
        "adopt": draw_adopt(jax.random.fold_in(key_list[7], 71), 0),
        "live": draw_live(jax.random.fold_in(key_list[7], 71), 0),
    }


def to_owner(by_processor, adoption):
    extra = (1,) * (by_processor.ndim - 3)
    plan_full = adoption.reshape(adoption.shape + extra)
    own_slot = by_processor[:, :, 0]
    adopted = by_processor[:, :, 1]
    from_right = jnp.roll(adopted, -1, axis=1)
    from_left = jnp.roll(adopted, 1, axis=1)
    return jnp.where(plan_full == 0, own_slot, jnp.where(plan_full == 1, from_right, from_left))

def to_processor(owned, adoption):
    extra = (1,) * (owned.ndim - 2)
    plan_full = adoption.reshape(adoption.shape + extra)
    own_slot = jnp.where(plan_full == 0, owned, jnp.zeros_like(owned))
    left_plan = jnp.roll(plan_full, 1, axis=1)
    right_plan = jnp.roll(plan_full, -1, axis=1)
    adopted = jnp.where(left_plan == 1, jnp.roll(owned, 1, axis=1), jnp.where(right_plan == -1, jnp.roll(owned, -1, axis=1), jnp.zeros_like(owned)))
    return jnp.stack([own_slot, adopted], axis=2)

def section_backward(inputs, grads, down, upper):
    hidden = jnp.einsum('sptd,sdr->sptr', inputs.astype(jnp.float32), down.astype(jnp.float32))
    gate_sigmoid = jax.nn.sigmoid(hidden)
    active = (hidden * gate_sigmoid).astype(jnp.bfloat16)
    coupled = jnp.einsum('sptd,sdr->sptr', grads.astype(jnp.float32), upper.astype(jnp.float32))
    inner_grad = (gate_sigmoid * (1.0 + hidden * (1.0 - gate_sigmoid)) * coupled).astype(jnp.bfloat16)
    returned = jnp.einsum('sptr,sdr->sptd', inner_grad.astype(jnp.float32), down.astype(jnp.float32))
    outflow = (grads.astype(jnp.float32) + returned).astype(jnp.bfloat16)
    return (active, outflow)

def reference(saved, incoming, head, down_weight, up_weight, adopt, live):
    relays = saved.shape[1]
    step_count = saved.shape[2]
    row_count = saved.shape[4]
    bottleneck = down_weight.shape[2]
    grads = to_owner(incoming, adopt[:, :, 0])
    grad_steps = []
    active_steps = []
    outflow = grads
    for step_index in range(step_count):
        inputs = to_owner(saved[:, :, step_index], adopt[:, :, step_index])
        active, outflow = section_backward(inputs, grads, down_weight, up_weight)
        grad_steps.append(grads)
        active_steps.append(active)
        if step_index + 1 < step_count:
            grads = jnp.concatenate([outflow[1:], head[step_index][None]], axis=0)
    leaving = to_processor(outflow, adopt[:, :, step_count - 1])
    norm_factor = 1.0 / math.sqrt(relays * step_count * row_count)
    grads_all = jnp.stack(grad_steps, axis=1)
    active_all = jnp.stack(active_steps, axis=1)
    live_float = live.astype(jnp.float32)

    def one_section(operands):
        plan_section, grads_section, active_section = operands
        partial_value = jnp.zeros((relays, grads_section.shape[-1], bottleneck), jnp.float32)
        for step_index in range(step_count):
            plan_now = plan_section[:, step_index][:, None, None]
            contribution = jnp.einsum('ptd,ptr->pdr', grads_section[step_index].astype(jnp.float32), active_section[step_index].astype(jnp.float32))
            zero = jnp.zeros_like(contribution)
            partial_value = partial_value + jnp.where(plan_now == 0, contribution, zero)
            partial_value = partial_value + jnp.roll(jnp.where(plan_now == 1, contribution, zero), 1, axis=0)
            partial_value = partial_value + jnp.roll(jnp.where(plan_now == -1, contribution, zero), -1, axis=0)
        masked = (partial_value * live_float[:, None, None]).astype(jnp.bfloat16)
        total = lax.optimization_barrier(jnp.sum(masked.astype(jnp.float32), axis=0)) * norm_factor
        return total.astype(jnp.bfloat16)
    totals = lax.map(one_section, (adopt, grads_all, active_all))
    return (leaving, totals)
```

```python
import functools
import math

import jax
import jax.numpy as jnp
from jax import lax
from jax.experimental import pallas as pl
from jax.experimental.pallas import tpu as pltpu
from jax.sharding import PartitionSpec as P

MESH = pl.DeviceIdType.MESH
F32, BF16 = jnp.float32, jnp.bfloat16
RIGHT, LEFT = 0, 1
INC, HID, LEAVE = 0, 1, 2


def kernel(S, N, K, T, D, R, NC,
           saved, incoming, head, wd, wu, adopt, live, leaving, grad,
           wdf, wuf, x, inc, inc_in, hacc, h_in, cacc, g, u, fac, outb, leave_in, rs_out, rs_in, plan,
           lsem, ws, wr, xs, xr, cs, cr, rss, rsr):
    H, blk = N // 2, D // N
    half, rows = blk // 2, K * T
    cols = D // NC
    per = cols // blk
    sec, me = lax.axis_index("section"), lax.axis_index("dp")
    right, left = lax.rem(me + 1, N), lax.rem(me + N - 1, N)
    below, above = lax.rem(sec + S - 1, S), lax.rem(sec + 1, S)
    side = ((sec, right), (sec, left))

    loads = [
        pltpu.make_async_copy(wd.at[0], wdf.at[me], lsem.at[0]),
        pltpu.make_async_copy(wu.at[0], wuf.at[me], lsem.at[1]),
        pltpu.make_async_copy(incoming.at[0, 0], inc, lsem.at[2]),
        pltpu.make_async_copy(adopt, plan, lsem.at[3]),
        pltpu.make_async_copy(saved.at[0, 0, :, 0], x.at[0], lsem.at[4]),
        pltpu.make_async_copy(saved.at[0, 0, :, 1], x.at[1], lsem.at[5]),
    ]
    for load in loads:
        load.start()
    heads = [pltpu.make_async_copy(head.at[k, 0], g.at[k + 1], lsem.at[6 + k]) for k in range(K - 1)]

    @pl.when(sec == S - 1)
    def _():
        for load in heads:
            load.start()

    barrier = pltpu.get_barrier_semaphore()
    for target in ((sec, left), (sec, right), (below, me), (above, me)):
        pl.semaphore_signal(barrier, inc=1, device_id=target, device_id_type=MESH)
    pl.semaphore_wait(barrier, 4)

    def remote(src, dst, send, recv, target):
        return pltpu.make_async_remote_copy(
            src_ref=src, dst_ref=dst, send_sem=send, recv_sem=recv, device_id=target, device_id_type=MESH
        )

    full = (wdf, wuf)

    def away(way, distance):
        return lax.rem(me + N - distance, N) if way == RIGHT else lax.rem(me + distance, N)

    def weight(w, way, hop, c, arriving):
        owner = away(way, hop if arriving else hop - 1)
        ref = full[w].at[owner, pl.ds(c * half, half)]
        return remote(ref, ref, ws.at[w, way, hop - 1, c], wr.at[w, way, hop - 1, c], side[way])

    def exchange(e, way, src, dst):
        return remote(src, dst.at[way], xs.at[e, way], xr.at[e, way], side[way])

    def add_h(b):
        columns = pl.ds(pl.multiple_of(b * blk, blk), blk)
        block = x[:, :, :, columns].reshape(2 * rows, blk)
        hacc[...] += jnp.dot(block, wdf[b], preferred_element_type=F32)

    def add_c(b):
        columns = pl.ds(pl.multiple_of(b * blk, blk), blk)
        cacc[...] += jnp.dot(g[0, :, columns], wuf[b], preferred_element_type=F32)

    def hops(w, add):
        def step(hop, _):
            for c in (0, 1):
                for way in (RIGHT, LEFT):
                    weight(w, way, hop - 1, c, True).wait_recv()
                    weight(w, way, hop, c, False).start()
            add(away(RIGHT, hop - 1))
            add(away(LEFT, hop - 1))
            return 0

        lax.fori_loop(2, H, step, 0)
        for c in (0, 1):
            for way in (RIGHT, LEFT):
                weight(w, way, H - 1, c, True).wait_recv()
                if c == way:
                    weight(w, way, H, c, False).start()

    def last_hop(w, add):
        add(away(RIGHT, H - 1))
        add(away(LEFT, H - 1))
        for way in (RIGHT, LEFT):
            weight(w, way, H, way, True).wait_recv()
        add(away(RIGHT, H))

    def first_hop(w):
        for c in (0, 1):
            for way in (RIGHT, LEFT):
                weight(w, way, 1, c, False).start()

    loads[0].wait()
    first_hop(0)
    loads[2].wait()
    inc_copies = [exchange(INC, way, inc.at[1], inc_in) for way in (RIGHT, LEFT)]
    for copy in inc_copies:
        copy.start()
    loads[1].wait()
    loads[3].wait()
    loads[4].wait()
    loads[5].wait()
    hacc[...] = jnp.zeros_like(hacc)
    add_h(me)
    hops(0, add_h)
    first_hop(1)
    last_hop(0, add_h)
    hid_copies = [exchange(HID, way, hacc.at[pl.ds(rows, rows)], h_in) for way in (RIGHT, LEFT)]
    for copy in hid_copies:
        copy.start()

    for copy in inc_copies:
        copy.wait_recv()
    offsets = [plan[me, k, sec] for k in range(K)]
    first = offsets[0]
    g[0] = jnp.where(first == 0, inc[0], jnp.where(first == 1, inc_in[LEFT], inc_in[RIGHT]))
    cacc[...] = jnp.zeros_like(cacc)
    add_c(me)
    hops(1, add_c)
    for copy in hid_copies:
        copy.wait_recv()
    for k in range(K):
        d = offsets[k]
        part = pl.ds(k * T, T)
        h = jnp.where(d == 0, hacc[part], jnp.where(d == 1, h_in[LEFT, part], h_in[RIGHT, part]))
        gate = jax.nn.sigmoid(h)
        fac[k] = gate * (1.0 + h * (1.0 - gate))
        joins = jnp.where(d == 0, live[me], jnp.where(d == 1, live[right], live[left]))
        u[part] = jnp.where(joins == 1, h * gate, 0.0).astype(BF16)
    last_hop(1, add_c)

    def chain(k, j):
        part = pl.ds(j * cols, cols)
        return remote(outb.at[k, :, part], g.at[k + 1, :, part], cs.at[k, j], cr.at[k, j], (below, me))

    def out_chunk(k, j, inner):
        part = pl.ds(j * cols, cols)
        back = lax.dot_general(
            inner, wdf[pl.ds(j * per, per)].reshape(cols, R), (((1,), (1,)), ((), ())), preferred_element_type=F32
        )
        outb[k, :, part] = (g[k, :, part].astype(F32) + back).astype(BF16)

    @pl.when(sec == S - 1)
    def _():
        for load in heads:
            load.wait()

    for k in range(K - 1):
        inner = (fac[k] * cacc[...]).astype(BF16)
        for j in range(NC):
            out_chunk(k, j, inner)

            @pl.when(sec > 0)
            def _():
                chain(k, j).start()

        total = jnp.zeros((T, R), F32)
        for j in range(NC):
            @pl.when(sec < S - 1)
            def _():
                chain(k, j).wait_recv()

            total += jnp.dot(
                g[k + 1, :, pl.ds(j * cols, cols)], wuf[pl.ds(j * per, per)].reshape(cols, R),
                preferred_element_type=F32,
            )
        cacc[...] = total

    def own(r):
        columns = pl.ds(pl.multiple_of(r * blk, blk), blk)
        return lax.dot_general(
            g[:, :, columns].reshape(rows, blk), u[...], (((0,), (0,)), ((), ())), preferred_element_type=F32
        )

    def ring_sum(way, step, c):
        part = pl.ds(c * half, half)
        return remote(
            rs_out.at[way, step - 1, part], rs_in.at[way, step - 1, part],
            rss.at[way, step - 1, c], rsr.at[way, step - 1, c], side[way],
        )

    def target(way, step):
        return away(1 - way, H + 1 - step)

    term = own(target(RIGHT, 1))
    for way in (RIGHT, LEFT):
        rs_out[way, 0, pl.ds(way * half, half)] = term[way * half : (way + 1) * half].astype(BF16)
        ring_sum(way, 1, way).start()

    inner = (fac[K - 1] * cacc[...]).astype(BF16)
    for j in range(NC):
        out_chunk(K - 1, j, inner)
    leave_copies = [exchange(LEAVE, way, outb.at[K - 1], leave_in) for way in (RIGHT, LEFT)]
    for copy in leave_copies:
        copy.start()

    for way in (RIGHT, LEFT):
        term = own(target(way, 2))
        for c in (way, 1 - way):
            part = pl.ds(c * half, half)
            value = term[c * half : (c + 1) * half]
            if c == way:
                ring_sum(way, 1, c).wait_recv()
                value = value + rs_in[way, 0, part].astype(F32)
            rs_out[way, 1, part] = value.astype(BF16)
            ring_sum(way, 2, c).start()

    def sum_step(step, _):
        terms = [own(target(way, step)) for way in (RIGHT, LEFT)]
        for c in (0, 1):
            part = pl.ds(c * half, half)
            for way in (RIGHT, LEFT):
                ring_sum(way, step - 1, c).wait_recv()
                value = terms[way][c * half : (c + 1) * half] + rs_in[way, step - 2, part].astype(F32)
                rs_out[way, step - 1, part] = value.astype(BF16)
                ring_sum(way, step, c).start()
        return 0

    lax.fori_loop(3, H + 1, sum_step, 0)

    last = offsets[K - 1]
    leaving[0, 0, 0] = jnp.where(last == 0, outb[K - 1], jnp.zeros((T, D), BF16))
    for copy in leave_copies:
        copy.wait_recv()
    leaving[0, 0, 1] = jnp.where(
        plan[left, K - 1, sec] == 1,
        leave_in[RIGHT],
        jnp.where(plan[right, K - 1, sec] == -1, leave_in[LEFT], jnp.zeros((T, D), BF16)),
    )

    scale = 1.0 / math.sqrt(N * K * T)
    term = own(me)
    for c in (0, 1):
        part = pl.ds(c * half, half)
        for way in (RIGHT, LEFT):
            ring_sum(way, H, c).wait_recv()
        total = term[c * half : (c + 1) * half]
        total = total + rs_in[RIGHT, H - 1, part].astype(F32) + rs_in[LEFT, H - 1, part].astype(F32)
        grad[0, part] = (total * scale).astype(BF16)

    def drain_weights(hop, _):
        for w in (0, 1):
            for way in (RIGHT, LEFT):
                for c in (0, 1):
                    weight(w, way, hop, c, False).wait_send()
        return 0

    lax.fori_loop(1, H, drain_weights, 0)
    for w in (0, 1):
        for way in (RIGHT, LEFT):
            weight(w, way, H, way, False).wait_send()
    for copy in inc_copies + hid_copies + leave_copies:
        copy.wait_send()

    @pl.when(sec > 0)
    def _():
        for k in range(K - 1):
            for j in range(NC):
                chain(k, j).wait_send()

    for way in (RIGHT, LEFT):
        ring_sum(way, 1, way).wait_send()

    def drain_sums(step, _):
        for way in (RIGHT, LEFT):
            for c in (0, 1):
                ring_sum(way, step, c).wait_send()
        return 0

    lax.fori_loop(2, H + 1, drain_sums, 0)


def solution(mesh):
    S, N = mesh.shape["section"], mesh.shape["dp"]

    def body(saved, incoming, head, wd, wu, adopt, live):
        _, _, K, _, T, D = saved.shape
        blk, R = wd.shape[1:]
        H, rows, NC = N // 2, K * T, 4
        anywhere = pl.BlockSpec(memory_space=pl.ANY)
        vmem = pl.BlockSpec(memory_space=pltpu.VMEM)
        dma = pltpu.SemaphoreType.DMA
        return pl.pallas_call(
            functools.partial(kernel, S, N, K, T, D, R, NC),
            out_shape=(
                jax.ShapeDtypeStruct((1, 1, 2, T, D), BF16),
                jax.ShapeDtypeStruct((1, blk, R), BF16),
            ),
            in_specs=[anywhere] * 6 + [pl.BlockSpec(memory_space=pltpu.SMEM)],
            out_specs=(vmem, vmem),
            scratch_shapes=[
                pltpu.VMEM((N, blk, R), BF16),
                pltpu.VMEM((N, blk, R), BF16),
                pltpu.VMEM((2, K, T, D), BF16),
                pltpu.VMEM((2, T, D), BF16),
                pltpu.VMEM((2, T, D), BF16),
                pltpu.VMEM((2 * rows, R), F32),
                pltpu.VMEM((2, rows, R), F32),
                pltpu.VMEM((T, R), F32),
                pltpu.VMEM((K, T, D), BF16),
                pltpu.VMEM((rows, R), BF16),
                pltpu.VMEM((K, T, R), F32),
                pltpu.VMEM((K, T, D), BF16),
                pltpu.VMEM((2, T, D), BF16),
                pltpu.VMEM((2, H, blk, R), BF16),
                pltpu.VMEM((2, H, blk, R), BF16),
                pltpu.SMEM((N, K, S), jnp.int32),
                dma((5 + K,)),
                dma((2, 2, H, 2)),
                dma((2, 2, H, 2)),
                dma((3, 2)),
                dma((3, 2)),
                dma((K - 1, NC)),
                dma((K - 1, NC)),
                dma((2, H, 2)),
                dma((2, H, 2)),
            ],
            compiler_params=pltpu.CompilerParams(
                collective_id=0, has_side_effects=True, vmem_limit_bytes=40 * 1024 * 1024
            ),
        )(saved, incoming, head, wd, wu, adopt.transpose(1, 2, 0), live)

    return jax.shard_map(
        body,
        mesh=mesh,
        in_specs=(
            P("section", "dp", None, None, None, None),
            P("section", "dp", None, None, None),
            P(None, "dp", None, None),
            P("section", "dp", None),
            P("section", "dp", None),
            P(),
            P(),
        ),
        out_specs=(P("section", "dp", None, None, None), P("section", "dp", None)),
        check_vma=False,
    )
```

```python
import functools
import math

import jax
import jax.numpy as jnp
from jax import lax
from jax.experimental import pallas as pl
from jax.experimental.pallas import tpu as pltpu
from jax.sharding import PartitionSpec as P

MESH = pl.DeviceIdType.MESH
F32, BF16 = jnp.float32, jnp.bfloat16
RIGHT, LEFT = 0, 1
INC, HID, LEAVE = 0, 1, 2
DOWN, UP = 0, 1


def kernel(S, N, K, T, D, R,
           saved, incoming, head, wd, wu, adopt, live, leaving, grad,
           wdf, wuf, x, inc, inc_in, hacc, hb, h_in, cacc, g, u, fac, outb, leave_in, rs_out, rs_in, plan,
           lsem, ws, wr, xs, xr, cs, cr, rss, rsr):
    H, blk = N // 2, D // N
    half, rows = blk // 2, K * T
    sec, me = lax.axis_index("section"), lax.axis_index("dp")
    right, left = lax.rem(me + 1, N), lax.rem(me + N - 1, N)
    below, above = lax.rem(sec + S - 1, S), lax.rem(sec + 1, S)
    side = ((sec, right), (sec, left))

    loads = [
        pltpu.make_async_copy(wd.at[0], wdf.at[me], lsem.at[0]),
        pltpu.make_async_copy(wu.at[0], wuf.at[me], lsem.at[1]),
        pltpu.make_async_copy(incoming.at[0, 0], inc, lsem.at[2]),
        pltpu.make_async_copy(adopt, plan, lsem.at[3]),
        pltpu.make_async_copy(saved.at[0, 0, :, 0], x.at[0], lsem.at[4]),
        pltpu.make_async_copy(saved.at[0, 0, :, 1], x.at[1], lsem.at[5]),
    ]
    for load in loads:
        load.start()
    heads = [pltpu.make_async_copy(head.at[k, 0], g.at[k + 1], lsem.at[6 + k]) for k in range(K - 1)]

    @pl.when(sec == S - 1)
    def _():
        for load in heads:
            load.start()

    barrier = pltpu.get_barrier_semaphore()
    for target in ((sec, left), (sec, right), (below, me), (above, me)):
        pl.semaphore_signal(barrier, inc=1, device_id=target, device_id_type=MESH)
    pl.semaphore_wait(barrier, 4)

    def remote(src, dst, send, recv, target):
        return pltpu.make_async_remote_copy(
            src_ref=src, dst_ref=dst, send_sem=send, recv_sem=recv, device_id=target, device_id_type=MESH
        )

    full = (wdf, wuf)

    def away(way, distance):
        return lax.rem(me + N - distance, N) if way == RIGHT else lax.rem(me + distance, N)

    def weight(w, way, hop, arriving):
        ref = full[w].at[away(way, hop if arriving else hop - 1)]
        if isinstance(hop, int) and hop == H:
            ref = ref.at[pl.ds(way * half, half)]
        return remote(ref, ref, ws.at[w, way, hop - 1], wr.at[w, way, hop - 1], side[way])

    def exchange(e, way, src, dst):
        return remote(src, dst.at[way], xs.at[e, way], xr.at[e, way], side[way])

    def block(b):
        return pl.ds(pl.multiple_of(b * blk, blk), blk)

    def add_h(b):
        inputs = x[:, :, :, block(b)].reshape(2 * rows, blk)
        hacc[...] += jnp.dot(inputs, wdf[b], preferred_element_type=F32)

    def add_c(b):
        cacc[...] += jnp.dot(g[0, :, block(b)], wuf[b], preferred_element_type=F32)

    def pass_on(w, hop):
        for way in (RIGHT, LEFT):
            if hop > 1:
                weight(w, way, hop - 1, True).wait_recv()
            if hop <= H:
                weight(w, way, hop, False).start()

    def add_blocks(w, hop):
        add = (add_h, add_c)[w]
        for way in (RIGHT, LEFT) if 1 < hop <= H else (RIGHT,):
            add(away(way, hop - 1))

    loads[0].wait()
    pass_on(DOWN, 1)
    loads[2].wait()
    inc_copies = [exchange(INC, way, inc.at[1], inc_in) for way in (RIGHT, LEFT)]
    for copy in inc_copies:
        copy.start()
    for load in (loads[1], loads[3], loads[4], loads[5]):
        load.wait()
    offsets = [plan[me, k, sec] for k in range(K)]
    hacc[...] = jnp.zeros_like(hacc)
    cacc[...] = jnp.zeros_like(cacc)
    add_blocks(DOWN, 1)
    for hop in range(2, H + 2):
        pass_on(DOWN, hop)
        add_blocks(DOWN, hop)
        if hop == 2:
            for copy in inc_copies:
                copy.wait_recv()
        if hop == H + 1:
            hb[...] = hacc[pl.ds(rows, rows)].astype(BF16)
            hid_copies = [exchange(HID, way, hb, h_in) for way in (RIGHT, LEFT)]
            for copy in hid_copies:
                copy.start()
        pass_on(UP, hop - 1)
        if hop == 2:
            d = offsets[0]
            g[0] = jnp.where(d == 0, inc[0], jnp.where(d == 1, inc_in[LEFT], inc_in[RIGHT]))
        add_blocks(UP, hop - 1)

    for copy in hid_copies:
        copy.wait_recv()
    for k in range(K):
        d = offsets[k]
        part = pl.ds(k * T, T)
        h = jnp.where(d == 0, hacc[part], jnp.where(d == 1, h_in[LEFT, part], h_in[RIGHT, part]).astype(F32))
        gate = jax.nn.sigmoid(h)
        fac[k] = gate * (1.0 + h * (1.0 - gate))
        joins = jnp.where(d == 0, live[me], jnp.where(d == 1, live[right], live[left]))
        u[part] = jnp.where(joins == 1, h * gate, 0.0).astype(BF16)
    pass_on(UP, H + 1)
    add_blocks(UP, H + 1)

    ring = [away(RIGHT, H)]
    for distance in range(H - 1, 0, -1):
        ring += [away(LEFT, distance), away(RIGHT, distance)]
    ring.append(me)

    def chain(k, i):
        part = block(ring[i])
        return remote(outb.at[k, :, part], g.at[k + 1, :, part], cs.at[k, i], cr.at[k, i], (below, me))

    def out_block(k, i, inner):
        part = block(ring[i])
        back = lax.dot_general(inner, wdf[ring[i]], (((1,), (1,)), ((), ())), preferred_element_type=F32)
        outb[k, :, part] = (g[k, :, part].astype(F32) + back).astype(BF16)

    def next_c(k, i):
        @pl.when(sec < S - 1)
        def _():
            chain(k, i).wait_recv()

        return jnp.dot(g[k + 1, :, block(ring[i])], wuf[ring[i]], preferred_element_type=F32)

    @pl.when(sec == S - 1)
    def _():
        for load in heads:
            load.wait()

    def send_out(k):
        inner = (fac[k] * cacc[...]).astype(BF16)
        for i in range(N):
            out_block(k, i, inner)

            @pl.when(sec > 0)
            def _():
                chain(k, i).start()

    for k in range(K - 2):
        send_out(k)
        total = next_c(k, 0)
        for i in range(1, N):
            total += next_c(k, i)
        cacc[...] = total

    def own(r, c):
        columns = pl.ds(pl.multiple_of(r * blk + c * half, half), half)
        return lax.dot_general(
            g[:, :, columns].reshape(rows, half), u[...], (((0,), (0,)), ((), ())), preferred_element_type=F32
        )

    def ring_sum(way, step, c):
        part = pl.ds(c * half, half)
        return remote(
            rs_out.at[way, step - 1, part], rs_in.at[way, step - 1, part],
            rss.at[way, step - 1, c], rsr.at[way, step - 1, c], side[way],
        )

    def sum_step(stream, step, fresh=False):
        pairs = [(way, way ^ stream) for way in (RIGHT, LEFT)]
        terms = [own(away(1 - way, H + 1 - step), c) for way, c in pairs]
        for (way, c), value in zip(pairs, terms):
            part = pl.ds(c * half, half)
            if not fresh:
                ring_sum(way, step - 1, c).wait_recv()
                value = value + rs_in[way, step - 2, part].astype(F32)
            rs_out[way, step - 1, part] = value.astype(BF16)
            ring_sum(way, step, c).start()

    send_out(K - 2)
    total = next_c(K - 2, 0)
    sum_step(0, 1, fresh=True)
    total += next_c(K - 2, 1)
    total += next_c(K - 2, 2)
    sum_step(1, 2, fresh=True)
    for i in range(3, N):
        total += next_c(K - 2, i)

    inner = (fac[K - 1] * total).astype(BF16)
    for i in range(N):
        out_block(K - 1, i, inner)
    leave_copies = [exchange(LEAVE, way, outb.at[K - 1], leave_in) for way in (RIGHT, LEFT)]
    for copy in leave_copies:
        copy.start()

    def sum_steps(step, _):
        sum_step(0, step)
        sum_step(1, step + 1)
        return 0

    lax.fori_loop(2, H, sum_steps, 0)
    sum_step(0, H)

    last = offsets[K - 1]
    leaving[0, 0, 0] = jnp.where(last == 0, outb[K - 1], jnp.zeros((T, D), BF16))
    for copy in leave_copies:
        copy.wait_recv()
    leaving[0, 0, 1] = jnp.where(
        plan[left, K - 1, sec] == 1,
        leave_in[RIGHT],
        jnp.where(plan[right, K - 1, sec] == -1, leave_in[LEFT], jnp.zeros((T, D), BF16)),
    )

    scale = 1.0 / math.sqrt(N * K * T)
    for c in (0, 1):
        part = pl.ds(c * half, half)
        total = own(me, c)
        for way in (RIGHT, LEFT):
            ring_sum(way, H, c).wait_recv()
            total = total + rs_in[way, H - 1, part].astype(F32)
        grad[0, part] = (total * scale).astype(BF16)

    for w in (DOWN, UP):
        for way in (RIGHT, LEFT):
            for hop in range(1, H + 1):
                weight(w, way, hop, False).wait_send()
    for copy in inc_copies + hid_copies + leave_copies:
        copy.wait_send()

    @pl.when(sec > 0)
    def _():
        for k in range(K - 1):
            for i in range(N):
                chain(k, i).wait_send()

    for way in (RIGHT, LEFT):
        ring_sum(way, 1, way).wait_send()

    def drain_sums(step, _):
        for way in (RIGHT, LEFT):
            for c in (0, 1):
                ring_sum(way, step, c).wait_send()
        return 0

    lax.fori_loop(2, H + 1, drain_sums, 0)


def solution(mesh):
    S, N = mesh.shape["section"], mesh.shape["dp"]

    def body(saved, incoming, head, wd, wu, adopt, live):
        _, _, K, _, T, D = saved.shape
        blk, R = wd.shape[1:]
        H, rows = N // 2, K * T
        anywhere = pl.BlockSpec(memory_space=pltpu.HBM)
        vmem = pl.BlockSpec(memory_space=pltpu.VMEM)
        dma = pltpu.SemaphoreType.DMA
        return pl.pallas_call(
            functools.partial(kernel, S, N, K, T, D, R),
            out_shape=(
                jax.ShapeDtypeStruct((1, 1, 2, T, D), BF16),
                jax.ShapeDtypeStruct((1, blk, R), BF16),
            ),
            in_specs=[anywhere] * 6 + [pl.BlockSpec(memory_space=pltpu.SMEM)],
            out_specs=(vmem, vmem),
            scratch_shapes=[
                pltpu.VMEM((N, blk, R), BF16),
                pltpu.VMEM((N, blk, R), BF16),
                pltpu.VMEM((2, K, T, D), BF16),
                pltpu.VMEM((2, T, D), BF16),
                pltpu.VMEM((2, T, D), BF16),
                pltpu.VMEM((2 * rows, R), F32),
                pltpu.VMEM((rows, R), BF16),
                pltpu.VMEM((2, rows, R), BF16),
                pltpu.VMEM((T, R), F32),
                pltpu.VMEM((K, T, D), BF16),
                pltpu.VMEM((rows, R), BF16),
                pltpu.VMEM((K, T, R), F32),
                pltpu.VMEM((K, T, D), BF16),
                pltpu.VMEM((2, T, D), BF16),
                pltpu.VMEM((2, H, blk, R), BF16),
                pltpu.VMEM((2, H, blk, R), BF16),
                pltpu.SMEM((N, K, S), jnp.int32),
                dma((5 + K,)),
                dma((2, 2, H)),
                dma((2, 2, H)),
                dma((3, 2)),
                dma((3, 2)),
                dma((K - 1, N)),
                dma((K - 1, N)),
                dma((2, H, 2)),
                dma((2, H, 2)),
            ],
            compiler_params=pltpu.CompilerParams(
                collective_id=0, has_side_effects=True, vmem_limit_bytes=60 * 1024 * 1024
            ),
        )(saved, incoming, head, wd, wu, adopt.transpose(1, 2, 0), live)

    return jax.shard_map(
        body,
        mesh=mesh,
        in_specs=(
            P("section", "dp", None, None, None, None),
            P("section", "dp", None, None, None),
            P(None, "dp", None, None),
            P("section", "dp", None),
            P("section", "dp", None),
            P(),
            P(),
        ),
        out_specs=(P("section", "dp", None, None, None), P("section", "dp", None)),
        check_vma=False,
    )
```

```python
import functools
import math

import jax
import jax.numpy as jnp
from jax import lax
from jax.experimental import pallas as pl
from jax.experimental.pallas import tpu as pltpu
from jax.sharding import PartitionSpec as P

MESH = pl.DeviceIdType.MESH
F32, BF16 = jnp.float32, jnp.bfloat16
RIGHT, LEFT = 0, 1
INC, HID, LEAVE = 0, 1, 2
DOWN, UP = 0, 1


def kernel(S, N, K, T, D, R,
           saved, incoming, head, wd, wu, adopt, live, leaving, grad,
           wdf, wuf, wda, x, inc, inc_in, hacc, hb, h_in, cacc, g, ga, u, fac, inner_out, inner_in, out, leave_in,
           rs_out, rs_in, plan, lsem, hsem, ws, wr, ds, dr, xs, xr, gs, gr, ns, nr, cs, cr, rss, rsr):
    H, blk = N // 2, D // N
    half, rows = blk // 2, K * T
    sec, me = lax.axis_index("section"), lax.axis_index("dp")
    right, left = lax.rem(me + 1, N), lax.rem(me + N - 1, N)
    below, above = lax.rem(sec + S - 1, S), lax.rem(sec + 1, S)
    side = ((sec, right), (sec, left))

    offset = [H] + [o for distance in range(H - 1, 0, -1) for o in (distance, -distance)] + [0]
    place = {o % N: i for i, o in enumerate(offset)}
    column = [lax.rem(me + o % N, N) for o in offset]

    def at(way, distance):
        return place[(-distance if way == RIGHT else distance) % N]

    def block(i):
        return pl.ds(pl.multiple_of(column[i] * blk, blk), blk)

    loads = [
        pltpu.make_async_copy(wd.at[0], wdf.at[N - 1], lsem.at[0]),
        pltpu.make_async_copy(wu.at[0], wuf.at[N - 1], lsem.at[1]),
        pltpu.make_async_copy(incoming.at[0, 0], inc, lsem.at[2]),
        pltpu.make_async_copy(adopt, plan, lsem.at[3]),
        pltpu.make_async_copy(saved.at[0, 0, :, 0], x.at[0], lsem.at[4]),
        pltpu.make_async_copy(saved.at[0, 0, :, 1], x.at[1], lsem.at[5]),
    ]
    for load in loads:
        load.start()
    def head_copy(k, i):
        return pltpu.make_async_copy(head.at[k, 0, :, block(i)], g.at[k + 1, i], hsem.at[k, i])

    @pl.when(sec == S - 1)
    def _():
        for k in range(K - 1):
            for i in range(N):
                head_copy(k, i).start()

    barrier = pltpu.get_barrier_semaphore()
    for target in ((sec, left), (sec, right), (below, me), (above, me)):
        pl.semaphore_signal(barrier, inc=1, device_id=target, device_id_type=MESH)
    pl.semaphore_wait(barrier, 4)

    def remote(src, dst, send, recv, target):
        return pltpu.make_async_remote_copy(
            src_ref=src, dst_ref=dst, send_sem=send, recv_sem=recv, device_id=target, device_id_type=MESH
        )

    full = (wdf, wuf)

    def weight(w, way, hop):
        src, dst = full[w].at[at(way, hop - 1)], full[w].at[at(way, hop)]
        if hop == H:
            src, dst = src.at[pl.ds(way * half, half)], dst.at[pl.ds(way * half, half)]
        return remote(src, dst, ws.at[w, way, hop - 1], wr.at[w, way, hop - 1], side[way])

    def exchange(e, way, src, dst):
        return remote(src, dst.at[way], xs.at[e, way], xr.at[e, way], side[way])

    def add_h(i):
        inputs = x[:, :, :, block(i)].reshape(2 * rows, blk)
        hacc[...] += jnp.dot(inputs, wdf[i], preferred_element_type=F32)

    def add_c(i):
        cacc[...] += jnp.dot(g[0, i], wuf[i], preferred_element_type=F32)

    def pass_on(w, hop):
        for way in (RIGHT, LEFT):
            if hop > 1:
                weight(w, way, hop - 1).wait_recv()
            if hop <= H:
                weight(w, way, hop).start()

    def arrived(hop):
        return [(way, at(way, hop - 1)) for way in ((RIGHT, LEFT) if 1 < hop <= H else (RIGHT,))]

    def add_blocks(w, hop):
        for _, i in arrived(hop):
            (add_h, add_c)[w](i)

    def lower(hop, way, i):
        return remote(wdf.at[i], wda.at[i], ds.at[hop - 1, way], dr.at[hop - 1, way], (below, me))

    def lower_blocks(hop):
        @pl.when(sec > 0)
        def _():
            for way, i in arrived(hop):
                lower(hop, way, i).start()

    loads[0].wait()
    pass_on(DOWN, 1)
    loads[2].wait()
    inc_copies = [exchange(INC, way, inc.at[1], inc_in) for way in (RIGHT, LEFT)]
    for copy in inc_copies:
        copy.start()
    for load in (loads[1], loads[3], loads[4], loads[5]):
        load.wait()
    offsets = [plan[me, k, sec] for k in range(K)]
    first_g = remote(g.at[0], ga.at[0], gs, gr, (below, me))
    hacc[...] = jnp.zeros_like(hacc)
    cacc[...] = jnp.zeros_like(cacc)
    lower_blocks(1)
    add_blocks(DOWN, 1)
    for hop in range(2, H + 2):
        pass_on(DOWN, hop)
        lower_blocks(hop)
        add_blocks(DOWN, hop)
        if hop == 2:
            for copy in inc_copies:
                copy.wait_recv()
        if hop == H + 1:
            hb[...] = hacc[pl.ds(rows, rows)].astype(BF16)
            hid_copies = [exchange(HID, way, hb, h_in) for way in (RIGHT, LEFT)]
            for copy in hid_copies:
                copy.start()
        pass_on(UP, hop - 1)
        if hop == 2:
            d = offsets[0]
            for i in range(N):
                part = block(i)
                g[0, i] = jnp.where(
                    d == 0, inc[0, :, part], jnp.where(d == 1, inc_in[LEFT, :, part], inc_in[RIGHT, :, part])
                )

            @pl.when(sec > 0)
            def _():
                first_g.start()

        add_blocks(UP, hop - 1)

    for copy in hid_copies:
        copy.wait_recv()
    for k in range(K):
        d = offsets[k]
        part = pl.ds(k * T, T)
        h = jnp.where(d == 0, hacc[part], jnp.where(d == 1, h_in[LEFT, part], h_in[RIGHT, part]).astype(F32))
        gate = jax.nn.sigmoid(h)
        fac[k] = gate * (1.0 + h * (1.0 - gate))
        joins = jnp.where(d == 0, live[me], jnp.where(d == 1, live[right], live[left]))
        u[part] = jnp.where(joins == 1, h * gate, 0.0).astype(BF16)
    pass_on(UP, H + 1)
    add_blocks(UP, H + 1)

    ends = sorted({0, 3, (3 + N) // 2, N})
    pieces = list(zip(ends[:-1], ends[1:]))

    def back(inner, weights):
        return lax.dot_general(inner, weights, (((1,), (1,)), ((), ())), preferred_element_type=F32)

    def chain(k, n):
        part = pl.ds(pieces[n][0], pieces[n][1] - pieces[n][0])
        return remote(g.at[k, part], ga.at[k, part], cs.at[k - 1, n], cr.at[k - 1, n], (below, me))

    def chain_inner(k):
        return remote(inner_out.at[k], inner_in.at[k], ns.at[k], nr.at[k], (below, me))

    def send_inner(k):
        inner_out[k] = (fac[k] * cacc[...]).astype(BF16)

        @pl.when(sec > 0)
        def _():
            chain_inner(k).start()

    def next_g(k, n):
        @pl.when(sec < S - 1)
        def _():
            if n == 0:
                chain_inner(k).wait_recv()
            if k > 0:
                chain(k, n).wait_recv()
            inner = inner_in[k]
            for i in range(*pieces[n]):
                g[k + 1, i] = (ga[k, i].astype(F32) + back(inner, wda[i])).astype(BF16)

        if k + 1 < K - 1:
            @pl.when(sec > 0)
            def _():
                chain(k + 1, n).start()

    def next_c(k):
        total = jnp.zeros((T, R), F32)
        for i in range(N):
            total += jnp.dot(g[k + 1, i], wuf[i], preferred_element_type=F32)
        cacc[...] = total

    send_inner(0)

    @pl.when(sec == S - 1)
    def _():
        for k in range(K - 1):
            for i in range(N):
                head_copy(k, i).wait()

    @pl.when(sec < S - 1)
    def _():
        first_g.wait_recv()
        for hop in range(1, H + 2):
            for way, i in arrived(hop):
                lower(hop, way, i).wait_recv()

    for k in range(K - 2):
        for n in range(len(pieces)):
            next_g(k, n)
        next_c(k)
        send_inner(k + 1)

    def own(i, c):
        return lax.dot_general(
            g[:, i, :, c * half : (c + 1) * half].reshape(rows, half), u[...], (((0,), (0,)), ((), ())),
            preferred_element_type=F32,
        )

    quarter = half // 2

    def ring_sum(way, step, q):
        part = pl.ds(q * quarter, quarter)
        return remote(
            rs_out.at[way, step - 1, part], rs_in.at[way, step - 1, part],
            rss.at[way, step - 1, q], rsr.at[way, step - 1, q], side[way],
        )

    def sum_step(stream, step, fresh=False):
        first = isinstance(step, int) and step == 1
        terms = [own(0 if first else 2 * step - 3 + way, way ^ stream) for way in (RIGHT, LEFT)]
        for n in (0, 1):
            for way in (RIGHT, LEFT):
                q = 2 * (way ^ stream) + n
                part = pl.ds(q * quarter, quarter)
                value = terms[way][n * quarter : (n + 1) * quarter]
                if not fresh:
                    ring_sum(way, step - 1, q).wait_recv()
                    value = value + rs_in[way, step - 2, part].astype(F32)
                rs_out[way, step - 1, part] = value.astype(BF16)
                ring_sum(way, step, q).start()

    next_g(K - 2, 0)
    sum_step(0, 1, True)
    sum_step(1, 2, True)
    for n in range(1, len(pieces)):
        next_g(K - 2, n)
    next_c(K - 2)

    inner = (fac[K - 1] * cacc[...]).astype(BF16)
    for i in range(N):
        out[i] = (g[K - 1, i].astype(F32) + back(inner, wdf[i])).astype(BF16)
    leave_copies = [exchange(LEAVE, way, out, leave_in) for way in (RIGHT, LEFT)]
    for copy in leave_copies:
        copy.start()

    def sum_steps(step, _):
        sum_step(0, step)
        sum_step(1, step + 1)
        return 0

    lax.fori_loop(2, H, sum_steps, 0)
    sum_step(0, H)

    here = offsets[K - 1] == 0
    from_left, from_right = plan[left, K - 1, sec] == 1, plan[right, K - 1, sec] == -1
    nothing = jnp.zeros((T, blk), BF16)
    for i in range(N):
        leaving[0, 0, 0, :, block(i)] = jnp.where(here, out[i], nothing)
    for copy in leave_copies:
        copy.wait_recv()
    for i, o in enumerate(offset):
        leaving[0, 0, 1, :, block(i)] = jnp.where(
            from_left,
            leave_in[RIGHT, place[(o + 1) % N]],
            jnp.where(from_right, leave_in[LEFT, place[(o - 1) % N]], nothing),
        )

    scale = 1.0 / math.sqrt(N * K * T)
    for c in (0, 1):
        total = own(N - 1, c)
        for n in (0, 1):
            q = 2 * c + n
            part = pl.ds(q * quarter, quarter)
            value = total[n * quarter : (n + 1) * quarter]
            for way in (RIGHT, LEFT):
                ring_sum(way, H, q).wait_recv()
                value = value + rs_in[way, H - 1, part].astype(F32)
            grad[0, part] = (value * scale).astype(BF16)

    for w in (DOWN, UP):
        for way in (RIGHT, LEFT):
            for hop in range(1, H + 1):
                weight(w, way, hop).wait_send()
    for copy in inc_copies + hid_copies + leave_copies:
        copy.wait_send()

    @pl.when(sec > 0)
    def _():
        first_g.wait_send()
        for hop in range(1, H + 2):
            for way, i in arrived(hop):
                lower(hop, way, i).wait_send()
        for k in range(K - 1):
            chain_inner(k).wait_send()
        for k in range(1, K - 1):
            for n in range(len(pieces)):
                chain(k, n).wait_send()

    for way in (RIGHT, LEFT):
        for n in (0, 1):
            ring_sum(way, 1, 2 * way + n).wait_send()

    def drain_sums(step, _):
        for way in (RIGHT, LEFT):
            for q in range(4):
                ring_sum(way, step, q).wait_send()
        return 0

    lax.fori_loop(2, H + 1, drain_sums, 0)


def solution(mesh):
    S, N = mesh.shape["section"], mesh.shape["dp"]

    def body(saved, incoming, head, wd, wu, adopt, live):
        _, _, K, _, T, D = saved.shape
        blk, R = wd.shape[1:]
        H, rows = N // 2, K * T
        anywhere = pl.BlockSpec(memory_space=pltpu.HBM)
        vmem = pl.BlockSpec(memory_space=pltpu.VMEM)
        dma = pltpu.SemaphoreType.DMA
        return pl.pallas_call(
            functools.partial(kernel, S, N, K, T, D, R),
            out_shape=(
                jax.ShapeDtypeStruct((1, 1, 2, T, D), BF16),
                jax.ShapeDtypeStruct((1, blk, R), BF16),
            ),
            in_specs=[anywhere] * 6 + [pl.BlockSpec(memory_space=pltpu.SMEM)],
            out_specs=(vmem, vmem),
            scratch_shapes=[
                pltpu.VMEM((N, blk, R), BF16),
                pltpu.VMEM((N, blk, R), BF16),
                pltpu.VMEM((N, blk, R), BF16),
                pltpu.VMEM((2, K, T, D), BF16),
                pltpu.VMEM((2, T, D), BF16),
                pltpu.VMEM((2, T, D), BF16),
                pltpu.VMEM((2 * rows, R), F32),
                pltpu.VMEM((rows, R), BF16),
                pltpu.VMEM((2, rows, R), BF16),
                pltpu.VMEM((T, R), F32),
                pltpu.VMEM((K, N, T, blk), BF16),
                pltpu.VMEM((K - 1, N, T, blk), BF16),
                pltpu.VMEM((rows, R), BF16),
                pltpu.VMEM((K, T, R), F32),
                pltpu.VMEM((K - 1, T, R), BF16),
                pltpu.VMEM((K - 1, T, R), BF16),
                pltpu.VMEM((N, T, blk), BF16),
                pltpu.VMEM((2, N, T, blk), BF16),
                pltpu.VMEM((2, H, blk, R), BF16),
                pltpu.VMEM((2, H, blk, R), BF16),
                pltpu.SMEM((N, K, S), jnp.int32),
                dma((6,)),
                dma((K - 1, N)),
                dma((2, 2, H)),
                dma((2, 2, H)),
                dma((H + 1, 2)),
                dma((H + 1, 2)),
                dma((3, 2)),
                dma((3, 2)),
                dma,
                dma,
                dma((K - 1,)),
                dma((K - 1,)),
                dma((K - 2, 3)),
                dma((K - 2, 3)),
                dma((2, H, 4)),
                dma((2, H, 4)),
            ],
            compiler_params=pltpu.CompilerParams(
                collective_id=0, has_side_effects=True, vmem_limit_bytes=60 * 1024 * 1024
            ),
        )(saved, incoming, head, wd, wu, adopt.transpose(1, 2, 0), live)

    return jax.shard_map(
        body,
        mesh=mesh,
        in_specs=(
            P("section", "dp", None, None, None, None),
            P("section", "dp", None, None, None),
            P(None, "dp", None, None),
            P("section", "dp", None),
            P("section", "dp", None),
            P(),
            P(),
        ),
        out_specs=(P("section", "dp", None, None, None), P("section", "dp", None)),
        check_vma=False,
    )
```

```python
import functools
import math

import jax
import jax.numpy as jnp
from jax import lax
from jax.experimental import pallas as pl
from jax.experimental.pallas import tpu as pltpu
from jax.sharding import PartitionSpec as P

MESH = pl.DeviceIdType.MESH
F32, BF16 = jnp.float32, jnp.bfloat16
RIGHT, LEFT = 0, 1
INC, HID, LEAVE = 0, 1, 2
DOWN, UP = 0, 1


def kernel(S, N, K, T, D, R,
           saved, incoming, head, wd, wu, adopt, live, leaving, grad,
           wdf, wuf, wda, x, inc, inc_in, hacc, hb, h_in, cacc, g, ga, u, fac, inner_out, inner_in, inner_side, spare, leave_in, pass_out, pass_in,
           rs_out, rs_in, plan, lsem, hsem, ws, wr, ds, dr, xs, xr, gs, gr, ns, nr, cs, cr, spsem, is_, ir, ps, pr, rss, rsr):
    H, blk = N // 2, D // N
    half, rows = blk // 2, K * T
    sec, me = lax.axis_index("section"), lax.axis_index("dp")
    right, left = lax.rem(me + 1, N), lax.rem(me + N - 1, N)
    below, above = lax.rem(sec + S - 1, S), lax.rem(sec + 1, S)
    side = ((sec, right), (sec, left))

    offset = [H] + [o for distance in range(H - 1, 0, -1) for o in (distance, -distance)] + [0]
    place = {o % N: i for i, o in enumerate(offset)}
    column = [lax.rem(me + o % N, N) for o in offset]

    def at(way, distance):
        return place[(-distance if way == RIGHT else distance) % N]

    def block(i):
        return pl.ds(pl.multiple_of(column[i] * blk, blk), blk)

    loads = [
        pltpu.make_async_copy(wd.at[0], wdf.at[N - 1], lsem.at[0]),
        pltpu.make_async_copy(wu.at[0], wuf.at[N - 1], lsem.at[1]),
        pltpu.make_async_copy(incoming.at[0, 0], inc, lsem.at[2]),
        pltpu.make_async_copy(adopt, plan, lsem.at[3]),
        pltpu.make_async_copy(saved.at[0, 0, :, 0], x.at[0], lsem.at[4]),
        pltpu.make_async_copy(saved.at[0, 0, :, 1], x.at[1], lsem.at[5]),
    ]
    for load in loads:
        load.start()
    def head_copy(k, i):
        return pltpu.make_async_copy(head.at[k, 0, :, block(i)], g.at[k + 1, i], hsem.at[k, i])

    @pl.when(sec == S - 1)
    def _():
        for k in range(K - 1):
            for i in range(N):
                head_copy(k, i).start()

    def spare_copy(i):
        return pltpu.make_async_copy(head.at[sec, 0, :, block(i)], spare.at[i], spsem.at[i])

    @pl.when(sec < K - 1)
    def _():
        for i in range(N):
            spare_copy(i).start()

    barrier = pltpu.get_barrier_semaphore()
    for target in ((sec, left), (sec, right), (below, me), (above, me)):
        pl.semaphore_signal(barrier, inc=1, device_id=target, device_id_type=MESH)
    pl.semaphore_wait(barrier, 4)

    def remote(src, dst, send, recv, target):
        return pltpu.make_async_remote_copy(
            src_ref=src, dst_ref=dst, send_sem=send, recv_sem=recv, device_id=target, device_id_type=MESH
        )

    full = (wdf, wuf)

    def weight(w, way, hop):
        src, dst = full[w].at[at(way, hop - 1)], full[w].at[at(way, hop)]
        if hop == H:
            src, dst = src.at[pl.ds(way * half, half)], dst.at[pl.ds(way * half, half)]
        return remote(src, dst, ws.at[w, way, hop - 1], wr.at[w, way, hop - 1], side[way])

    def exchange(e, way, src, dst):
        return remote(src, dst.at[way], xs.at[e, way], xr.at[e, way], side[way])

    def add_h(i):
        inputs = x[:, :, :, block(i)].reshape(2 * rows, blk)
        hacc[...] += jnp.dot(inputs, wdf[i], preferred_element_type=F32)

    def add_c(i):
        cacc[...] += jnp.dot(g[0, i], wuf[i], preferred_element_type=F32)

    def pass_on(w, hop):
        for way in (RIGHT, LEFT):
            if hop > 1:
                weight(w, way, hop - 1).wait_recv()
            if hop <= H:
                weight(w, way, hop).start()

    def arrived(hop):
        return [(way, at(way, hop - 1)) for way in ((RIGHT, LEFT) if 1 < hop <= H else (RIGHT,))]

    def add_blocks(w, hop):
        for _, i in arrived(hop):
            (add_h, add_c)[w](i)

    def lower(hop, way, i):
        return remote(wdf.at[i], wda.at[i], ds.at[hop - 1, way], dr.at[hop - 1, way], (below, me))

    def lower_blocks(hop):
        @pl.when(sec > 0)
        def _():
            for way, i in arrived(hop):
                lower(hop, way, i).start()

    loads[0].wait()
    pass_on(DOWN, 1)
    loads[2].wait()
    inc_copies = [exchange(INC, way, inc.at[1], inc_in) for way in (RIGHT, LEFT)]
    for copy in inc_copies:
        copy.start()
    for load in (loads[1], loads[3], loads[4], loads[5]):
        load.wait()
    offsets = [plan[me, k, sec] for k in range(K)]
    first_g = remote(g.at[0], ga.at[0], gs, gr, (below, me))
    hacc[...] = jnp.zeros_like(hacc)
    cacc[...] = jnp.zeros_like(cacc)
    lower_blocks(1)
    add_blocks(DOWN, 1)
    for hop in range(2, H + 2):
        pass_on(DOWN, hop)
        lower_blocks(hop)
        add_blocks(DOWN, hop)
        if hop == 2:
            for copy in inc_copies:
                copy.wait_recv()
        if hop == H + 1:
            hb[...] = hacc[pl.ds(rows, rows)].astype(BF16)
            hid_copies = [exchange(HID, way, hb, h_in) for way in (RIGHT, LEFT)]
            for copy in hid_copies:
                copy.start()
        pass_on(UP, hop - 1)
        if hop == 2:
            d = offsets[0]
            for i in range(N):
                part = block(i)
                g[0, i] = jnp.where(
                    d == 0, inc[0, :, part], jnp.where(d == 1, inc_in[LEFT, :, part], inc_in[RIGHT, :, part])
                )

            @pl.when(sec > 0)
            def _():
                first_g.start()

        add_blocks(UP, hop - 1)

    for copy in hid_copies:
        copy.wait_recv()
    for k in range(K):
        d = offsets[k]
        part = pl.ds(k * T, T)
        h = jnp.where(d == 0, hacc[part], jnp.where(d == 1, h_in[LEFT, part], h_in[RIGHT, part]).astype(F32))
        gate = jax.nn.sigmoid(h)
        fac[k] = gate * (1.0 + h * (1.0 - gate))
        joins = jnp.where(d == 0, live[me], jnp.where(d == 1, live[right], live[left]))
        u[part] = jnp.where(joins == 1, h * gate, 0.0).astype(BF16)
    pass_on(UP, H + 1)
    add_blocks(UP, H + 1)

    ends = sorted({0, 3, (3 + N) // 2, N})
    pieces = list(zip(ends[:-1], ends[1:]))

    def back(inner, weights):
        return lax.dot_general(inner, weights, (((1,), (1,)), ((), ())), preferred_element_type=F32)

    def chain(k, n):
        part = pl.ds(pieces[n][0], pieces[n][1] - pieces[n][0])
        return remote(g.at[k, part], ga.at[k, part], cs.at[k - 1, n], cr.at[k - 1, n], (below, me))

    def chain_inner(k):
        return remote(inner_out.at[k], inner_in.at[k], ns.at[k], nr.at[k], (below, me))

    def side_inner(k, way):
        return remote(inner_out.at[k], inner_side.at[k, way], is_.at[k, way], ir.at[k, way], side[way])

    def send_inner(k):
        inner_out[k] = (fac[k] * cacc[...]).astype(BF16)
        if k < K - 1:
            @pl.when(sec > 0)
            def _():
                chain_inner(k).start()

        for way in (RIGHT, LEFT):
            side_inner(k, way).start()

    def next_g(k, n):
        @pl.when(sec < S - 1)
        def _():
            if n == 0:
                chain_inner(k).wait_recv()
            if k > 0:
                chain(k, n).wait_recv()
            inner = inner_in[k]
            for i in range(*pieces[n]):
                g[k + 1, i] = (ga[k, i].astype(F32) + back(inner, wda[i])).astype(BF16)

        if k + 1 < K - 1:
            @pl.when(sec > 0)
            def _():
                chain(k + 1, n).start()

    def next_c(k):
        total = jnp.zeros((T, R), F32)
        for i in range(N):
            total += jnp.dot(g[k + 1, i], wuf[i], preferred_element_type=F32)
        cacc[...] = total

    def origin(way, src):
        return exchange(LEAVE, way, src, leave_in)

    send_inner(0)

    @pl.when(sec < K - 1)
    def _():
        for i in range(N):
            spare_copy(i).wait()
        for way in (RIGHT, LEFT):
            origin(way, spare).start()

    @pl.when(sec >= K - 1)
    def _():
        for way in (RIGHT, LEFT):
            origin(way, g.at[0]).start()

    def passing(k):
        return remote(pass_out.at[k], pass_in.at[k], ps.at[k], pr.at[k], (below, me))

    def leave_step(k):
        behind = K - 1 - k
        aim = lax.rem(sec + S - behind, S)
        from_left, from_right = plan[left, K - 1, aim] == 1, plan[right, K - 1, aim] == -1
        for way in (RIGHT, LEFT):
            side_inner(k, way).wait_recv()
        inner = jnp.where(from_left, inner_side[k, RIGHT], inner_side[k, LEFT])
        inner = jnp.where(sec >= behind, inner, jnp.zeros_like(inner))
        if k == 0:
            for way in (RIGHT, LEFT):
                origin(way, spare).wait_recv()
        else:
            passing(k - 1).wait_recv()
        for i, o in enumerate(offset):
            if k == 0:
                before = jnp.where(from_left, leave_in[RIGHT, place[(o + 1) % N]], leave_in[LEFT, place[(o - 1) % N]])
            else:
                before = pass_in[k - 1, i]
            value = (before.astype(F32) + back(inner, wdf[i])).astype(BF16)
            if k < K - 1:
                pass_out[k, i] = value
            else:
                nothing = jnp.zeros((T, blk), BF16)
                leaving[0, 0, 1, :, block(i)] = jnp.where(from_left, value, jnp.where(from_right, value, nothing))
        if k < K - 1:
            passing(k).start()

    @pl.when(sec == S - 1)
    def _():
        for k in range(K - 1):
            for i in range(N):
                head_copy(k, i).wait()

    @pl.when(sec < S - 1)
    def _():
        first_g.wait_recv()
        for hop in range(1, H + 2):
            for way, i in arrived(hop):
                lower(hop, way, i).wait_recv()

    for k in range(K - 2):
        for n in range(len(pieces)):
            next_g(k, n)
        next_c(k)
        send_inner(k + 1)

    def own(i, c):
        return lax.dot_general(
            g[:, i, :, c * half : (c + 1) * half].reshape(rows, half), u[...], (((0,), (0,)), ((), ())),
            preferred_element_type=F32,
        )

    quarter = half // 2

    def ring_sum(way, step, q):
        part = pl.ds(q * quarter, quarter)
        return remote(
            rs_out.at[way, step - 1, part], rs_in.at[way, step - 1, part],
            rss.at[way, step - 1, q], rsr.at[way, step - 1, q], side[way],
        )

    def sum_step(stream, step, fresh=False):
        first = isinstance(step, int) and step == 1
        terms = [own(0 if first else 2 * step - 3 + way, way ^ stream) for way in (RIGHT, LEFT)]
        for n in (0, 1):
            for way in (RIGHT, LEFT):
                q = 2 * (way ^ stream) + n
                part = pl.ds(q * quarter, quarter)
                value = terms[way][n * quarter : (n + 1) * quarter]
                if not fresh:
                    ring_sum(way, step - 1, q).wait_recv()
                    value = value + rs_in[way, step - 2, part].astype(F32)
                rs_out[way, step - 1, part] = value.astype(BF16)
                ring_sum(way, step, q).start()

    next_g(K - 2, 0)
    sum_step(0, 1, True)
    sum_step(1, 2, True)
    for n in range(1, len(pieces)):
        next_g(K - 2, n)
    next_c(K - 2)

    send_inner(K - 1)
    here = offsets[K - 1] == 0
    for i in range(N):
        value = (g[K - 1, i].astype(F32) + back(inner_out[K - 1], wdf[i])).astype(BF16)
        leaving[0, 0, 0, :, block(i)] = jnp.where(here, value, jnp.zeros((T, blk), BF16))
    leave_step(0)

    def sum_steps(step, _):
        sum_step(0, step)
        sum_step(1, step + 1)
        return 0

    steps = [min(2 + n * (H - 2) // (K - 1), H) for n in range(K)]
    for k in range(1, K):
        lax.fori_loop(steps[k - 1], steps[k], sum_steps, 0)
        leave_step(k)
    sum_step(0, H)

    scale = 1.0 / math.sqrt(N * K * T)
    for c in (0, 1):
        total = own(N - 1, c)
        for n in (0, 1):
            q = 2 * c + n
            part = pl.ds(q * quarter, quarter)
            value = total[n * quarter : (n + 1) * quarter]
            for way in (RIGHT, LEFT):
                ring_sum(way, H, q).wait_recv()
                value = value + rs_in[way, H - 1, part].astype(F32)
            grad[0, part] = (value * scale).astype(BF16)

    for w in (DOWN, UP):
        for way in (RIGHT, LEFT):
            for hop in range(1, H + 1):
                weight(w, way, hop).wait_send()
    for copy in inc_copies + hid_copies:
        copy.wait_send()
    for way in (RIGHT, LEFT):
        origin(way, spare).wait_send()
        for k in range(K):
            side_inner(k, way).wait_send()
    for k in range(K - 1):
        passing(k).wait_send()

    @pl.when(sec > 0)
    def _():
        first_g.wait_send()
        for hop in range(1, H + 2):
            for way, i in arrived(hop):
                lower(hop, way, i).wait_send()
        for k in range(K - 1):
            chain_inner(k).wait_send()
        for k in range(1, K - 1):
            for n in range(len(pieces)):
                chain(k, n).wait_send()

    for way in (RIGHT, LEFT):
        for n in (0, 1):
            ring_sum(way, 1, 2 * way + n).wait_send()

    def drain_sums(step, _):
        for way in (RIGHT, LEFT):
            for q in range(4):
                ring_sum(way, step, q).wait_send()
        return 0

    lax.fori_loop(2, H + 1, drain_sums, 0)


def hand_over(leaving, grad, leaving_out, grad_out):
    leaving_out[...] = leaving[...]
    grad_out[...] = grad[...]


def solution(mesh):
    S, N = mesh.shape["section"], mesh.shape["dp"]

    def body(saved, incoming, head, wd, wu, adopt, live):
        _, _, K, _, T, D = saved.shape
        blk, R = wd.shape[1:]
        H, rows = N // 2, K * T
        anywhere = pl.BlockSpec(memory_space=pltpu.HBM)
        vmem = pl.BlockSpec(memory_space=pltpu.VMEM)
        dma = pltpu.SemaphoreType.DMA
        results = pl.pallas_call(
            functools.partial(kernel, S, N, K, T, D, R),
            out_shape=(
                jax.ShapeDtypeStruct((1, 1, 2, T, D), BF16),
                jax.ShapeDtypeStruct((1, blk, R), BF16),
            ),
            in_specs=[anywhere] * 6 + [pl.BlockSpec(memory_space=pltpu.SMEM)],
            out_specs=(vmem, vmem),
            scratch_shapes=[
                pltpu.VMEM((N, blk, R), BF16),
                pltpu.VMEM((N, blk, R), BF16),
                pltpu.VMEM((N, blk, R), BF16),
                pltpu.VMEM((2, K, T, D), BF16),
                pltpu.VMEM((2, T, D), BF16),
                pltpu.VMEM((2, T, D), BF16),
                pltpu.VMEM((2 * rows, R), F32),
                pltpu.VMEM((rows, R), BF16),
                pltpu.VMEM((2, rows, R), BF16),
                pltpu.VMEM((T, R), F32),
                pltpu.VMEM((K, N, T, blk), BF16),
                pltpu.VMEM((K - 1, N, T, blk), BF16),
                pltpu.VMEM((rows, R), BF16),
                pltpu.VMEM((K, T, R), F32),
                pltpu.VMEM((K, T, R), BF16),
                pltpu.VMEM((K - 1, T, R), BF16),
                pltpu.VMEM((K, 2, T, R), BF16),
                pltpu.VMEM((N, T, blk), BF16),
                pltpu.VMEM((2, N, T, blk), BF16),
                pltpu.VMEM((K - 1, N, T, blk), BF16),
                pltpu.VMEM((K - 1, N, T, blk), BF16),
                pltpu.VMEM((2, H, blk, R), BF16),
                pltpu.VMEM((2, H, blk, R), BF16),
                pltpu.SMEM((N, K, S), jnp.int32),
                dma((6,)),
                dma((K - 1, N)),
                dma((2, 2, H)),
                dma((2, 2, H)),
                dma((H + 1, 2)),
                dma((H + 1, 2)),
                dma((3, 2)),
                dma((3, 2)),
                dma,
                dma,
                dma((K - 1,)),
                dma((K - 1,)),
                dma((K - 2, 3)),
                dma((K - 2, 3)),
                dma((N,)),
                dma((K, 2)),
                dma((K, 2)),
                dma((K - 1,)),
                dma((K - 1,)),
                dma((2, H, 4)),
                dma((2, H, 4)),
            ],
            compiler_params=pltpu.CompilerParams(
                collective_id=0, has_side_effects=True, vmem_limit_bytes=60 * 1024 * 1024
            ),
        )(saved, incoming, head, wd, wu, adopt.transpose(1, 2, 0), live)
        return pl.pallas_call(
            hand_over,
            out_shape=tuple(jax.ShapeDtypeStruct(r.shape, r.dtype) for r in results),
            in_specs=[vmem] * 2,
            out_specs=(vmem, vmem),
        )(*results)

    return jax.shard_map(
        body,
        mesh=mesh,
        in_specs=(
            P("section", "dp", None, None, None, None),
            P("section", "dp", None, None, None),
            P(None, "dp", None, None),
            P("section", "dp", None),
            P("section", "dp", None),
            P(),
            P(),
        ),
        out_specs=(P("section", "dp", None, None, None), P("section", "dp", None)),
        check_vma=False,
    )
```

```python
import functools
import math

import jax
import jax.numpy as jnp
from jax import lax
from jax.experimental import pallas as pl
from jax.experimental.pallas import tpu as pltpu
from jax.sharding import PartitionSpec as P

MESH = pl.DeviceIdType.MESH
F32, BF16 = jnp.float32, jnp.bfloat16
RIGHT, LEFT = 0, 1
INC, HID, LEAVE = 0, 1, 2
DOWN, UP = 0, 1


def kernel(S, N, K, T, D, R,
           saved, incoming, head, wd, wu, adopt, live, leaving, grad,
           wdf, wuf, wda, x, inc, inc_in, hacc, hb, h_in, cacc, above_c, mix, g, ga, u, fac, inner_out, inner_in, inner_side, spare, leave_in, pass_out, pass_in, part_back,
           rs_out, rs_in, plan, lsem, hsem, ws, wr, ds, dr, xs, xr, gs, gr, ns, nr, cs, cr, spsem, is_, ir, ps, pr, rss, rsr):
    H, blk = N // 2, D // N
    half, rows = blk // 2, K * T
    sec, me = lax.axis_index("section"), lax.axis_index("dp")
    right, left = lax.rem(me + 1, N), lax.rem(me + N - 1, N)
    below, above = lax.rem(sec + S - 1, S), lax.rem(sec + 1, S)
    side = ((sec, right), (sec, left))

    offset = [H] + [o for distance in range(H - 1, 0, -1) for o in (distance, -distance)] + [0]
    place = {o % N: i for i, o in enumerate(offset)}
    column = [lax.rem(me + o % N, N) for o in offset]

    def at(way, distance):
        return place[(-distance if way == RIGHT else distance) % N]

    def block(i):
        return pl.ds(pl.multiple_of(column[i] * blk, blk), blk)

    loads = [
        pltpu.make_async_copy(wd.at[0], wdf.at[N - 1], lsem.at[0]),
        pltpu.make_async_copy(wu.at[0], wuf.at[N - 1], lsem.at[1]),
        pltpu.make_async_copy(incoming.at[0, 0], inc, lsem.at[2]),
        pltpu.make_async_copy(adopt, plan, lsem.at[3]),
        pltpu.make_async_copy(saved.at[0, 0, :, 0], x.at[0], lsem.at[4]),
        pltpu.make_async_copy(saved.at[0, 0, :, 1], x.at[1], lsem.at[5]),
    ]
    for load in loads:
        load.start()
    def head_copy(k, i):
        return pltpu.make_async_copy(head.at[k, 0, :, block(i)], g.at[k + 1, i], hsem.at[k, i])

    @pl.when(sec == S - 1)
    def _():
        for k in range(K - 1):
            for i in range(N):
                head_copy(k, i).start()

    def spare_copy(i):
        return pltpu.make_async_copy(head.at[sec, 0, :, block(i)], spare.at[i], spsem.at[i])

    @pl.when(sec < K - 1)
    def _():
        for i in range(N):
            spare_copy(i).start()

    barrier = pltpu.get_barrier_semaphore()
    for target in ((sec, left), (sec, right), (below, me), (above, me)):
        pl.semaphore_signal(barrier, inc=1, device_id=target, device_id_type=MESH)
    pl.semaphore_wait(barrier, 4)

    def remote(src, dst, send, recv, target):
        return pltpu.make_async_remote_copy(
            src_ref=src, dst_ref=dst, send_sem=send, recv_sem=recv, device_id=target, device_id_type=MESH
        )

    full = (wdf, wuf)

    def weight(w, way, hop):
        src, dst = full[w].at[at(way, hop - 1)], full[w].at[at(way, hop)]
        if hop == H:
            src, dst = src.at[pl.ds(way * half, half)], dst.at[pl.ds(way * half, half)]
        return remote(src, dst, ws.at[w, way, hop - 1], wr.at[w, way, hop - 1], side[way])

    def exchange(e, way, src, dst):
        return remote(src, dst.at[way], xs.at[e, way], xr.at[e, way], side[way])

    def add_h(i):
        inputs = x[:, :, :, block(i)].reshape(2 * rows, blk)
        hacc[...] += jnp.dot(inputs, wdf[i], preferred_element_type=F32)

    def add_c(i):
        cacc[...] += jnp.dot(g[0, i], wuf[i], preferred_element_type=F32)

    def pass_on(w, hop):
        for way in (RIGHT, LEFT):
            if hop > 1:
                weight(w, way, hop - 1).wait_recv()
            if hop <= H:
                weight(w, way, hop).start()

    def arrived(hop):
        return [(way, at(way, hop - 1)) for way in ((RIGHT, LEFT) if 1 < hop <= H else (RIGHT,))]

    def add_blocks(w, hop):
        for _, i in arrived(hop):
            (add_h, add_c)[w](i)

    def lower(hop, way, i):
        return remote(wdf.at[i], wda.at[i], ds.at[hop - 1, way], dr.at[hop - 1, way], (below, me))

    def add_mix(hop):
        @pl.when(sec < S - 1)
        def _():
            for way, i in arrived(hop):
                lower(hop, way, i).wait_recv()
                mix[...] += lax.dot_general(
                    wda[i], wuf[i], (((0,), (0,)), ((), ())), preferred_element_type=F32
                )

    def add_above(hop):
        @pl.when(sec < S - 1)
        def _():
            for _, i in arrived(hop):
                above_c[...] += jnp.dot(ga[0, i], wuf[i], preferred_element_type=F32)

    def lower_blocks(hop):
        @pl.when(sec > 0)
        def _():
            for way, i in arrived(hop):
                lower(hop, way, i).start()

    loads[0].wait()
    pass_on(DOWN, 1)
    loads[2].wait()
    inc_copies = [exchange(INC, way, inc.at[1], inc_in) for way in (RIGHT, LEFT)]
    for copy in inc_copies:
        copy.start()
    for load in (loads[1], loads[3], loads[4], loads[5]):
        load.wait()
    offsets = [plan[me, k, sec] for k in range(K)]
    first_g = remote(g.at[0], ga.at[0], gs, gr, (below, me))
    hacc[...] = jnp.zeros_like(hacc)
    cacc[...] = jnp.zeros_like(cacc)
    mix[...] = jnp.zeros_like(mix)
    above_c[...] = jnp.zeros_like(above_c)
    lower_blocks(1)
    add_blocks(DOWN, 1)
    for hop in range(2, H + 2):
        pass_on(DOWN, hop)
        lower_blocks(hop)
        add_blocks(DOWN, hop)
        if hop == 2:
            for copy in inc_copies:
                copy.wait_recv()
        if hop == H + 1:
            hb[...] = hacc[pl.ds(rows, rows)].astype(BF16)
            hid_copies = [exchange(HID, way, hb, h_in) for way in (RIGHT, LEFT)]
            for copy in hid_copies:
                copy.start()
        pass_on(UP, hop - 1)
        if hop == 2:
            d = offsets[0]
            for i in range(N):
                part = block(i)
                g[0, i] = jnp.where(
                    d == 0, inc[0, :, part], jnp.where(d == 1, inc_in[LEFT, :, part], inc_in[RIGHT, :, part])
                )

            @pl.when(sec > 0)
            def _():
                first_g.start()

        add_blocks(UP, hop - 1)
        if hop > 3:
            add_mix(hop - 3)
        if hop == min(5, H + 1):
            @pl.when(sec < S - 1)
            def _():
                first_g.wait_recv()

            for earlier in range(1, hop - 1):
                add_above(earlier)
        if hop >= min(5, H + 1):
            add_above(hop - 1)

    for copy in hid_copies:
        copy.wait_recv()
    for k in range(K):
        d = offsets[k]
        part = pl.ds(k * T, T)
        h = jnp.where(d == 0, hacc[part], jnp.where(d == 1, h_in[LEFT, part], h_in[RIGHT, part]).astype(F32))
        gate = jax.nn.sigmoid(h)
        fac[k] = gate * (1.0 + h * (1.0 - gate))
        joins = jnp.where(d == 0, live[me], jnp.where(d == 1, live[right], live[left]))
        u[part] = jnp.where(joins == 1, h * gate, 0.0).astype(BF16)
    for hop in range(H - 1, H + 1):
        add_mix(hop)
    pass_on(UP, H + 1)
    add_blocks(UP, H + 1)
    add_above(H + 1)
    add_mix(H + 1)

    ends = sorted({0, 3, (3 + N) // 2, N})
    pieces = list(zip(ends[:-1], ends[1:]))

    def back(inner, weights):
        return lax.dot_general(inner, weights, (((1,), (1,)), ((), ())), preferred_element_type=F32)

    def chain(k, n):
        part = pl.ds(pieces[n][0], pieces[n][1] - pieces[n][0])
        return remote(g.at[k, part], ga.at[k, part], cs.at[k - 1, n], cr.at[k - 1, n], (below, me))

    def chain_inner(k):
        return remote(inner_out.at[k], inner_in.at[k], ns.at[k], nr.at[k], (below, me))

    def side_inner(k, way):
        return remote(inner_out.at[k], inner_side.at[k, way], is_.at[k, way], ir.at[k, way], side[way])

    def send_inner(k):
        inner_out[k] = (fac[k] * cacc[...]).astype(BF16)
        if k < K - 1:
            @pl.when(sec > 0)
            def _():
                chain_inner(k).start()

        for way in (RIGHT, LEFT):
            side_inner(k, way).start()

    def next_g(k, n):
        @pl.when(sec < S - 1)
        def _():
            if k > 0:
                chain(k, n).wait_recv()
            inner = inner_in[k]
            for i in range(*pieces[n]):
                g[k + 1, i] = (ga[k, i].astype(F32) + back(inner, wda[i])).astype(BF16)
            if 0 < k < K - 2:
                total = above_c[...] if n > 0 else jnp.zeros((T, R), F32)
                for i in range(*pieces[n]):
                    total += jnp.dot(ga[k, i], wuf[i], preferred_element_type=F32)
                above_c[...] = total

        if k + 1 < K - 1:
            @pl.when(sec > 0)
            def _():
                chain(k + 1, n).start()

    def next_c(k):
        total = jnp.zeros((T, R), F32)
        for i in range(N):
            total += jnp.dot(g[k + 1, i], wuf[i], preferred_element_type=F32)
        cacc[...] = total

    def origin(way, src):
        return exchange(LEAVE, way, src, leave_in)

    send_inner(0)

    @pl.when(sec < K - 1)
    def _():
        for i in range(N):
            spare_copy(i).wait()
        for way in (RIGHT, LEFT):
            origin(way, spare).start()

    @pl.when(sec >= K - 1)
    def _():
        for way in (RIGHT, LEFT):
            origin(way, g.at[0]).start()

    def passing(k):
        return remote(pass_out.at[k], pass_in.at[k], ps.at[k], pr.at[k], (below, me))

    def adopted(k):
        behind = K - 1 - k
        aim = lax.rem(sec + S - behind, S)
        from_left, from_right = plan[left, K - 1, aim] == 1, plan[right, K - 1, aim] == -1
        for way in (RIGHT, LEFT):
            side_inner(k, way).wait_recv()
        inner = jnp.where(from_left, inner_side[k, RIGHT], inner_side[k, LEFT])
        return from_left, from_right, jnp.where(sec >= behind, inner, jnp.zeros_like(inner))

    nothing = jnp.zeros((T, blk), BF16)

    def leave_first():
        picks = [adopted(k) for k in range(K - 1)]
        inner = jnp.concatenate([inner_out[K - 1]] + [pick[2] for pick in picks], axis=0)
        from_left = picks[0][0]
        here = offsets[K - 1] == 0
        for way in (RIGHT, LEFT):
            origin(way, spare).wait_recv()
        for i, o in enumerate(offset):
            parts = back(inner, wdf[i])
            own_out = (g[K - 1, i].astype(F32) + parts[:T]).astype(BF16)
            leaving[0, 0, 0, :, block(i)] = jnp.where(here, own_out, nothing)
            before = jnp.where(from_left, leave_in[RIGHT, place[(o + 1) % N]], leave_in[LEFT, place[(o - 1) % N]])
            pass_out[0, i] = (before.astype(F32) + parts[T : 2 * T]).astype(BF16)
            for k in range(1, K - 1):
                part_back[k - 1, i] = parts[(k + 1) * T : (k + 2) * T]
        passing(0).start()

    def leave_step(k):
        if k == K - 1:
            from_left, from_right, inner = adopted(k)
        passing(k - 1).wait_recv()
        for i in range(N):
            before = pass_in[k - 1, i].astype(F32)
            if k < K - 1:
                pass_out[k, i] = (before + part_back[k - 1, i]).astype(BF16)
            else:
                value = (before + back(inner, wdf[i])).astype(BF16)
                leaving[0, 0, 1, :, block(i)] = jnp.where(from_left, value, jnp.where(from_right, value, nothing))
        if k < K - 1:
            passing(k).start()

    @pl.when(sec == S - 1)
    def _():
        for k in range(K - 1):
            for i in range(N):
                head_copy(k, i).wait()

    def wait_inner(k):
        @pl.when(sec < S - 1)
        def _():
            chain_inner(k).wait_recv()

    def mixed_c(k):
        @pl.when(sec < S - 1)
        def _():
            cacc[...] = above_c[...] + jnp.dot(inner_in[k], mix[...].astype(BF16), preferred_element_type=F32)

        @pl.when(sec == S - 1)
        def _():
            next_c(k)

    for k in range(K - 2):
        wait_inner(k)
        if k == 0:
            mixed_c(k)
            send_inner(k + 1)
        for n in range(len(pieces)):
            next_g(k, n)
        if k > 0:
            mixed_c(k)
            send_inner(k + 1)
    wait_inner(K - 2)

    def own(i, c):
        return lax.dot_general(
            g[:, i, :, c * half : (c + 1) * half].reshape(rows, half), u[...], (((0,), (0,)), ((), ())),
            preferred_element_type=F32,
        )

    quarter = half // 2

    def ring_sum(way, step, q):
        part = pl.ds(q * quarter, quarter)
        return remote(
            rs_out.at[way, step - 1, part], rs_in.at[way, step - 1, part],
            rss.at[way, step - 1, q], rsr.at[way, step - 1, q], side[way],
        )

    def sum_step(stream, step, fresh=False):
        first = isinstance(step, int) and step == 1
        terms = [own(0 if first else 2 * step - 3 + way, way ^ stream) for way in (RIGHT, LEFT)]
        for n in (0, 1):
            for way in (RIGHT, LEFT):
                q = 2 * (way ^ stream) + n
                part = pl.ds(q * quarter, quarter)
                value = terms[way][n * quarter : (n + 1) * quarter]
                if not fresh:
                    ring_sum(way, step - 1, q).wait_recv()
                    value = value + rs_in[way, step - 2, part].astype(F32)
                rs_out[way, step - 1, part] = value.astype(BF16)
                ring_sum(way, step, q).start()

    next_g(K - 2, 0)
    sum_step(0, 1, True)
    sum_step(1, 2, True)
    for n in range(1, len(pieces)):
        next_g(K - 2, n)
    next_c(K - 2)

    send_inner(K - 1)
    leave_first()

    def sum_steps(step, _):
        sum_step(0, step)
        sum_step(1, step + 1)
        return 0

    steps = [min(2 + n * (H - 2) // (K - 1), H) for n in range(K)]
    for k in range(1, K):
        lax.fori_loop(steps[k - 1], steps[k], sum_steps, 0)
        leave_step(k)
    sum_step(0, H)

    scale = 1.0 / math.sqrt(N * K * T)
    for c in (0, 1):
        total = own(N - 1, c)
        for n in (0, 1):
            q = 2 * c + n
            part = pl.ds(q * quarter, quarter)
            value = total[n * quarter : (n + 1) * quarter]
            for way in (RIGHT, LEFT):
                ring_sum(way, H, q).wait_recv()
                value = value + rs_in[way, H - 1, part].astype(F32)
            grad[0, part] = (value * scale).astype(BF16)

    for w in (DOWN, UP):
        for way in (RIGHT, LEFT):
            for hop in range(1, H + 1):
                weight(w, way, hop).wait_send()
    for copy in inc_copies + hid_copies:
        copy.wait_send()
    for way in (RIGHT, LEFT):
        origin(way, spare).wait_send()
        for k in range(K):
            side_inner(k, way).wait_send()
    for k in range(K - 1):
        passing(k).wait_send()

    @pl.when(sec > 0)
    def _():
        first_g.wait_send()
        for hop in range(1, H + 2):
            for way, i in arrived(hop):
                lower(hop, way, i).wait_send()
        for k in range(K - 1):
            chain_inner(k).wait_send()
        for k in range(1, K - 1):
            for n in range(len(pieces)):
                chain(k, n).wait_send()

    for way in (RIGHT, LEFT):
        for n in (0, 1):
            ring_sum(way, 1, 2 * way + n).wait_send()

    def drain_sums(step, _):
        for way in (RIGHT, LEFT):
            for q in range(4):
                ring_sum(way, step, q).wait_send()
        return 0

    lax.fori_loop(2, H + 1, drain_sums, 0)


def hand_over(leaving, grad, leaving_out, grad_out):
    leaving_out[...] = leaving[...]
    grad_out[...] = grad[...]


def solution(mesh):
    S, N = mesh.shape["section"], mesh.shape["dp"]

    def body(saved, incoming, head, wd, wu, adopt, live):
        _, _, K, _, T, D = saved.shape
        blk, R = wd.shape[1:]
        H, rows = N // 2, K * T
        anywhere = pl.BlockSpec(memory_space=pltpu.HBM)
        vmem = pl.BlockSpec(memory_space=pltpu.VMEM)
        dma = pltpu.SemaphoreType.DMA
        results = pl.pallas_call(
            functools.partial(kernel, S, N, K, T, D, R),
            out_shape=(
                jax.ShapeDtypeStruct((1, 1, 2, T, D), BF16),
                jax.ShapeDtypeStruct((1, blk, R), BF16),
            ),
            in_specs=[anywhere] * 6 + [pl.BlockSpec(memory_space=pltpu.SMEM)],
            out_specs=(vmem, vmem),
            scratch_shapes=[
                pltpu.VMEM((N, blk, R), BF16),
                pltpu.VMEM((N, blk, R), BF16),
                pltpu.VMEM((N, blk, R), BF16),
                pltpu.VMEM((2, K, T, D), BF16),
                pltpu.VMEM((2, T, D), BF16),
                pltpu.VMEM((2, T, D), BF16),
                pltpu.VMEM((2 * rows, R), F32),
                pltpu.VMEM((rows, R), BF16),
                pltpu.VMEM((2, rows, R), BF16),
                pltpu.VMEM((T, R), F32),
                pltpu.VMEM((T, R), F32),
                pltpu.VMEM((R, R), F32),
                pltpu.VMEM((K, N, T, blk), BF16),
                pltpu.VMEM((K - 1, N, T, blk), BF16),
                pltpu.VMEM((rows, R), BF16),
                pltpu.VMEM((K, T, R), F32),
                pltpu.VMEM((K, T, R), BF16),
                pltpu.VMEM((K - 1, T, R), BF16),
                pltpu.VMEM((K, 2, T, R), BF16),
                pltpu.VMEM((N, T, blk), BF16),
                pltpu.VMEM((2, N, T, blk), BF16),
                pltpu.VMEM((K - 1, N, T, blk), BF16),
                pltpu.VMEM((K - 1, N, T, blk), BF16),
                pltpu.VMEM((K - 2, N, T, blk), F32),
                pltpu.VMEM((2, H, blk, R), BF16),
                pltpu.VMEM((2, H, blk, R), BF16),
                pltpu.SMEM((N, K, S), jnp.int32),
                dma((6,)),
                dma((K - 1, N)),
                dma((2, 2, H)),
                dma((2, 2, H)),
                dma((H + 1, 2)),
                dma((H + 1, 2)),
                dma((3, 2)),
                dma((3, 2)),
                dma,
                dma,
                dma((K - 1,)),
                dma((K - 1,)),
                dma((K - 2, 3)),
                dma((K - 2, 3)),
                dma((N,)),
                dma((K, 2)),
                dma((K, 2)),
                dma((K - 1,)),
                dma((K - 1,)),
                dma((2, H, 4)),
                dma((2, H, 4)),
            ],
            compiler_params=pltpu.CompilerParams(
                collective_id=0, has_side_effects=True, vmem_limit_bytes=60 * 1024 * 1024
            ),
        )(saved, incoming, head, wd, wu, adopt.transpose(1, 2, 0), live)
        return pl.pallas_call(
            hand_over,
            out_shape=tuple(jax.ShapeDtypeStruct(r.shape, r.dtype) for r in results),
            in_specs=[vmem] * 2,
            out_specs=(vmem, vmem),
        )(*results)

    return jax.shard_map(
        body,
        mesh=mesh,
        in_specs=(
            P("section", "dp", None, None, None, None),
            P("section", "dp", None, None, None),
            P(None, "dp", None, None),
            P("section", "dp", None),
            P("section", "dp", None),
            P(),
            P(),
        ),
        out_specs=(P("section", "dp", None, None, None), P("section", "dp", None)),
        check_vma=False,
    )
```

```python
import functools
import math

import jax
import jax.numpy as jnp
from jax import lax
from jax.experimental import pallas as pl
from jax.experimental.pallas import tpu as pltpu
from jax.sharding import PartitionSpec as P

MESH = pl.DeviceIdType.MESH
F32, BF16 = jnp.float32, jnp.bfloat16
RIGHT, LEFT = 0, 1
INC, HID, LEAVE = 0, 1, 2
DOWN, UP = 0, 1


def kernel(S, N, K, T, D, R,
           saved, incoming, head, wd, wu, adopt, live, leaving, grad,
           wdf, wuf, wda, x, inc, inc_in, hacc, hb, h_in, cacc, above_c, mix, g, ga, u, fac, inner_out, inner_in, inner_side, spare, leave_in, pass_out, pass_in, part_back,
           rs_out, rs_in, plan, lsem, hsem, ws, wr, ds, dr, xs, xr, gs, gr, ns, nr, cs, cr, spsem, is_, ir, ps, pr, rss, rsr):
    H, blk = N // 2, D // N
    half, rows = blk // 2, K * T
    sec, me = lax.axis_index("section"), lax.axis_index("dp")
    right, left = lax.rem(me + 1, N), lax.rem(me + N - 1, N)
    below, above = lax.rem(sec + S - 1, S), lax.rem(sec + 1, S)
    side = ((sec, right), (sec, left))

    offset = [H] + [o for distance in range(H - 1, 0, -1) for o in (distance, -distance)] + [0]
    place = {o % N: i for i, o in enumerate(offset)}
    column = [lax.rem(me + o % N, N) for o in offset]

    def at(way, distance):
        return place[(-distance if way == RIGHT else distance) % N]

    def block(i):
        return pl.ds(pl.multiple_of(column[i] * blk, blk), blk)

    loads = [
        pltpu.make_async_copy(wd.at[0], wdf.at[N - 1], lsem.at[0]),
        pltpu.make_async_copy(wu.at[0], wuf.at[N - 1], lsem.at[1]),
        pltpu.make_async_copy(incoming.at[0, 0], inc, lsem.at[2]),
        pltpu.make_async_copy(adopt, plan, lsem.at[3]),
        pltpu.make_async_copy(saved.at[0, 0, :, 0], x.at[0], lsem.at[4]),
        pltpu.make_async_copy(saved.at[0, 0, :, 1], x.at[1], lsem.at[5]),
    ]
    for load in loads:
        load.start()
    def head_copy(k, i):
        return pltpu.make_async_copy(head.at[k, 0, :, block(i)], g.at[k + 1, i], hsem.at[k, i])

    @pl.when(sec == S - 1)
    def _():
        for k in range(K - 1):
            for i in range(N):
                head_copy(k, i).start()

    def spare_copy(i):
        return pltpu.make_async_copy(head.at[sec, 0, :, block(i)], spare.at[i], spsem.at[i])

    @pl.when(sec < K - 1)
    def _():
        for i in range(N):
            spare_copy(i).start()

    barrier = pltpu.get_barrier_semaphore()
    for target in ((sec, left), (sec, right), (below, me), (above, me)):
        pl.semaphore_signal(barrier, inc=1, device_id=target, device_id_type=MESH)
    pl.semaphore_wait(barrier, 4)

    def remote(src, dst, send, recv, target):
        return pltpu.make_async_remote_copy(
            src_ref=src, dst_ref=dst, send_sem=send, recv_sem=recv, device_id=target, device_id_type=MESH
        )

    full = (wdf, wuf)

    def weight(w, way, hop):
        src, dst = full[w].at[at(way, hop - 1)], full[w].at[at(way, hop)]
        if hop == H:
            src, dst = src.at[pl.ds(way * half, half)], dst.at[pl.ds(way * half, half)]
        return remote(src, dst, ws.at[w, way, hop - 1], wr.at[w, way, hop - 1], side[way])

    def exchange(e, way, src, dst):
        return remote(src, dst.at[way], xs.at[e, way], xr.at[e, way], side[way])

    def add_h(i):
        inputs = x[:, :, :, block(i)].reshape(2 * rows, blk)
        hacc[...] += jnp.dot(inputs, wdf[i], preferred_element_type=F32)

    def add_c(i):
        cacc[...] += jnp.dot(g[0, i], wuf[i], preferred_element_type=F32)

    def pass_on(w, hop):
        for way in (RIGHT, LEFT):
            if hop > 1:
                weight(w, way, hop - 1).wait_recv()
            if hop <= H:
                weight(w, way, hop).start()

    def arrived(hop):
        return [(way, at(way, hop - 1)) for way in ((RIGHT, LEFT) if 1 < hop <= H else (RIGHT,))]

    def add_blocks(w, hop):
        for _, i in arrived(hop):
            (add_h, add_c)[w](i)

    def lower(hop, way, i):
        return remote(wdf.at[i], wda.at[i], ds.at[hop - 1, way], dr.at[hop - 1, way], (below, me))

    def add_mix(hop):
        @pl.when(sec < S - 1)
        def _():
            for way, i in arrived(hop):
                lower(hop, way, i).wait_recv()
                mix[...] += lax.dot_general(
                    wda[i], wuf[i], (((0,), (0,)), ((), ())), preferred_element_type=F32
                )

    def add_above(hop):
        @pl.when(sec < S - 1)
        def _():
            for _, i in arrived(hop):
                above_c[...] += jnp.dot(ga[0, i], wuf[i], preferred_element_type=F32)

    def lower_blocks(hop):
        @pl.when(sec > 0)
        def _():
            for way, i in arrived(hop):
                lower(hop, way, i).start()

    loads[0].wait()
    pass_on(DOWN, 1)
    loads[2].wait()
    inc_copies = [exchange(INC, way, inc.at[1], inc_in) for way in (RIGHT, LEFT)]
    for copy in inc_copies:
        copy.start()
    for load in (loads[1], loads[3], loads[4], loads[5]):
        load.wait()
    offsets = [plan[me, k, sec] for k in range(K)]
    first_g = remote(g.at[0], ga.at[0], gs, gr, (below, me))
    hacc[...] = jnp.zeros_like(hacc)
    cacc[...] = jnp.zeros_like(cacc)
    mix[...] = jnp.zeros_like(mix)
    above_c[...] = jnp.zeros_like(above_c)
    lower_blocks(1)
    add_blocks(DOWN, 1)
    for hop in range(2, H + 2):
        pass_on(DOWN, hop)
        lower_blocks(hop)
        add_blocks(DOWN, hop)
        if hop == 2:
            for copy in inc_copies:
                copy.wait_recv()
        if hop == H + 1:
            hb[...] = hacc[pl.ds(rows, rows)].astype(BF16)
            hid_copies = [exchange(HID, way, hb, h_in) for way in (RIGHT, LEFT)]
            for copy in hid_copies:
                copy.start()
        pass_on(UP, hop - 1)
        if hop == 2:
            d = offsets[0]
            for i in range(N):
                part = block(i)
                g[0, i] = jnp.where(
                    d == 0, inc[0, :, part], jnp.where(d == 1, inc_in[LEFT, :, part], inc_in[RIGHT, :, part])
                )

            @pl.when(sec > 0)
            def _():
                first_g.start()

        add_blocks(UP, hop - 1)
        if hop > 3:
            add_mix(hop - 3)
        if hop == min(5, H + 1):
            @pl.when(sec < S - 1)
            def _():
                first_g.wait_recv()

            for earlier in range(1, hop - 1):
                add_above(earlier)
        if hop >= min(5, H + 1):
            add_above(hop - 1)

    for copy in hid_copies:
        copy.wait_recv()
    for k in range(K):
        d = offsets[k]
        part = pl.ds(k * T, T)
        h = jnp.where(d == 0, hacc[part], jnp.where(d == 1, h_in[LEFT, part], h_in[RIGHT, part]).astype(F32))
        gate = jax.nn.sigmoid(h)
        fac[k] = gate * (1.0 + h * (1.0 - gate))
        joins = jnp.where(d == 0, live[me], jnp.where(d == 1, live[right], live[left]))
        u[part] = jnp.where(joins == 1, h * gate, 0.0).astype(BF16)
    for hop in range(H - 1, H + 1):
        add_mix(hop)
    pass_on(UP, H + 1)
    add_blocks(UP, H + 1)
    add_above(H + 1)
    add_mix(H + 1)

    ends = sorted({0, 3, (3 + N) // 2, N})
    pieces = list(zip(ends[:-1], ends[1:]))

    def back(inner, weights):
        return lax.dot_general(inner, weights, (((1,), (1,)), ((), ())), preferred_element_type=F32)

    def chain(k, n):
        part = pl.ds(pieces[n][0], pieces[n][1] - pieces[n][0])
        return remote(g.at[k, part], ga.at[k, part], cs.at[k - 1, n], cr.at[k - 1, n], (below, me))

    def chain_inner(k):
        return remote(inner_out.at[k], inner_in.at[k], ns.at[k], nr.at[k], (below, me))

    def side_inner(k, way):
        return remote(inner_out.at[k], inner_side.at[k, way], is_.at[k, way], ir.at[k, way], side[way])

    def send_inner(k):
        inner_out[k] = (fac[k] * cacc[...]).astype(BF16)
        if k < K - 1:
            @pl.when(sec > 0)
            def _():
                chain_inner(k).start()

        for way in (RIGHT, LEFT):
            side_inner(k, way).start()

    def next_g(k, n):
        @pl.when(sec < S - 1)
        def _():
            if k > 0:
                chain(k, n).wait_recv()
            inner = inner_in[k]
            for i in range(*pieces[n]):
                g[k + 1, i] = (ga[k, i].astype(F32) + back(inner, wda[i])).astype(BF16)
            if 0 < k < K - 2:
                total = above_c[...] if n > 0 else jnp.zeros((T, R), F32)
                for i in range(*pieces[n]):
                    total += jnp.dot(ga[k, i], wuf[i], preferred_element_type=F32)
                above_c[...] = total

        if k + 1 < K - 1:
            @pl.when(sec > 0)
            def _():
                chain(k + 1, n).start()

    def next_c(k):
        total = jnp.zeros((T, R), F32)
        for i in range(N):
            total += jnp.dot(g[k + 1, i], wuf[i], preferred_element_type=F32)
        cacc[...] = total

    def origin(way, src):
        return exchange(LEAVE, way, src, leave_in)

    send_inner(0)

    @pl.when(sec < K - 1)
    def _():
        for i in range(N):
            spare_copy(i).wait()
        for way in (RIGHT, LEFT):
            origin(way, spare).start()

    @pl.when(sec >= K - 1)
    def _():
        for way in (RIGHT, LEFT):
            origin(way, g.at[0]).start()

    def passing(k):
        return remote(pass_out.at[k], pass_in.at[k], ps.at[k], pr.at[k], (below, me))

    def adopted(k):
        behind = K - 1 - k
        aim = lax.rem(sec + S - behind, S)
        from_left, from_right = plan[left, K - 1, aim] == 1, plan[right, K - 1, aim] == -1
        for way in (RIGHT, LEFT):
            side_inner(k, way).wait_recv()
        inner = jnp.where(from_left, inner_side[k, RIGHT], inner_side[k, LEFT])
        return from_left, from_right, jnp.where(sec >= behind, inner, jnp.zeros_like(inner))

    nothing = jnp.zeros((T, blk), BF16)

    def leave_first():
        picks = [adopted(k) for k in range(K - 1)]
        inner = jnp.concatenate([inner_out[K - 1]] + [pick[2] for pick in picks], axis=0)
        from_left = picks[0][0]
        here = offsets[K - 1] == 0
        for way in (RIGHT, LEFT):
            origin(way, spare).wait_recv()
        for i, o in enumerate(offset):
            parts = back(inner, wdf[i])
            own_out = (g[K - 1, i].astype(F32) + parts[:T]).astype(BF16)
            leaving[0, 0, 0, :, block(i)] = jnp.where(here, own_out, nothing)
            before = jnp.where(from_left, leave_in[RIGHT, place[(o + 1) % N]], leave_in[LEFT, place[(o - 1) % N]])
            pass_out[0, i] = (before.astype(F32) + parts[T : 2 * T]).astype(BF16)
            for k in range(1, K - 1):
                part_back[k - 1, i] = parts[(k + 1) * T : (k + 2) * T]
        passing(0).start()

    def leave_step(k):
        if k == K - 1:
            from_left, from_right, inner = adopted(k)
        passing(k - 1).wait_recv()
        for i in range(N):
            before = pass_in[k - 1, i].astype(F32)
            if k < K - 1:
                pass_out[k, i] = (before + part_back[k - 1, i]).astype(BF16)
            else:
                value = (before + back(inner, wdf[i])).astype(BF16)
                leaving[0, 0, 1, :, block(i)] = jnp.where(from_left, value, jnp.where(from_right, value, nothing))
        if k < K - 1:
            passing(k).start()

    @pl.when(sec == S - 1)
    def _():
        for k in range(K - 1):
            for i in range(N):
                head_copy(k, i).wait()

    def wait_inner(k):
        @pl.when(sec < S - 1)
        def _():
            chain_inner(k).wait_recv()

    def mixed_c(k):
        @pl.when(sec < S - 1)
        def _():
            cacc[...] = above_c[...] + jnp.dot(inner_in[k], mix[...].astype(BF16), preferred_element_type=F32)

        @pl.when(sec == S - 1)
        def _():
            next_c(k)

    for k in range(K - 2):
        wait_inner(k)
        if k == 0:
            mixed_c(k)
            send_inner(k + 1)
        for n in range(len(pieces)):
            next_g(k, n)
        if k > 0:
            mixed_c(k)
            send_inner(k + 1)
    wait_inner(K - 2)

    def own(i, c):
        return lax.dot_general(
            g[:, i, :, c * half : (c + 1) * half].reshape(rows, half), u[...], (((0,), (0,)), ((), ())),
            preferred_element_type=F32,
        )

    quarter = half // 2

    def ring_sum(way, step, q):
        part = pl.ds(q * quarter, quarter)
        return remote(
            rs_out.at[way, step - 1, part], rs_in.at[way, step - 1, part],
            rss.at[way, step - 1, q], rsr.at[way, step - 1, q], side[way],
        )

    def sum_step(stream, step, fresh=False):
        first = isinstance(step, int) and step == 1
        terms = [own(0 if first else 2 * step - 3 + way, way ^ stream) for way in (RIGHT, LEFT)]
        for n in (0, 1):
            for way in (RIGHT, LEFT):
                q = 2 * (way ^ stream) + n
                part = pl.ds(q * quarter, quarter)
                value = terms[way][n * quarter : (n + 1) * quarter]
                if not fresh:
                    ring_sum(way, step - 1, q).wait_recv()
                    value = value + rs_in[way, step - 2, part].astype(F32)
                rs_out[way, step - 1, part] = value.astype(BF16)
                ring_sum(way, step, q).start()

    next_g(K - 2, 0)
    sum_step(0, 1, True)
    sum_step(1, 2, True)
    for n in range(1, len(pieces)):
        next_g(K - 2, n)
    next_c(K - 2)

    send_inner(K - 1)
    leave_first()

    def sum_steps(step, _):
        sum_step(0, step)
        sum_step(1, step + 1)
        return 0

    steps = [min(2 + n * (H - 2) // (K - 1), H) for n in range(K)]
    for k in range(1, K):
        lax.fori_loop(steps[k - 1], steps[k], sum_steps, 0)
        leave_step(k)
    sum_step(0, H)

    for w in (DOWN, UP):
        for way in (RIGHT, LEFT):
            for hop in range(1, H + 1):
                weight(w, way, hop).wait_send()
    for copy in inc_copies + hid_copies:
        copy.wait_send()
    for way in (RIGHT, LEFT):
        origin(way, spare).wait_send()
        for k in range(K):
            side_inner(k, way).wait_send()
    for k in range(K - 1):
        passing(k).wait_send()

    @pl.when(sec > 0)
    def _():
        first_g.wait_send()
        for hop in range(1, H + 2):
            for way, i in arrived(hop):
                lower(hop, way, i).wait_send()
        for k in range(K - 1):
            chain_inner(k).wait_send()
        for k in range(1, K - 1):
            for n in range(len(pieces)):
                chain(k, n).wait_send()

    for way in (RIGHT, LEFT):
        for n in (0, 1):
            ring_sum(way, 1, 2 * way + n).wait_send()

    def drain_sums(step, _):
        for way in (RIGHT, LEFT):
            for q in range(4):
                ring_sum(way, step, q).wait_send()
        return 0

    lax.fori_loop(2, H + 1, drain_sums, 0)

    scale = 1.0 / math.sqrt(N * K * T)
    for c in (0, 1):
        total = own(N - 1, c)
        for n in (0, 1):
            q = 2 * c + n
            part = pl.ds(q * quarter, quarter)
            value = total[n * quarter : (n + 1) * quarter]
            for way in (RIGHT, LEFT):
                ring_sum(way, H, q).wait_recv()
                value = value + rs_in[way, H - 1, part].astype(F32)
            grad[0, part] = (value * scale).astype(BF16)


def hand_over(leaving, grad, leaving_out, grad_out):
    leaving_out[...] = leaving[...]
    grad_out[...] = grad[...]


def solution(mesh):
    S, N = mesh.shape["section"], mesh.shape["dp"]

    def body(saved, incoming, head, wd, wu, adopt, live):
        _, _, K, _, T, D = saved.shape
        blk, R = wd.shape[1:]
        H, rows = N // 2, K * T
        anywhere = pl.BlockSpec(memory_space=pltpu.HBM)
        vmem = pl.BlockSpec(memory_space=pltpu.VMEM)
        dma = pltpu.SemaphoreType.DMA
        results = pl.pallas_call(
            functools.partial(kernel, S, N, K, T, D, R),
            out_shape=(
                jax.ShapeDtypeStruct((1, 1, 2, T, D), BF16),
                jax.ShapeDtypeStruct((1, blk, R), BF16),
            ),
            in_specs=[anywhere] * 6 + [pl.BlockSpec(memory_space=pltpu.SMEM)],
            out_specs=(vmem, vmem),
            scratch_shapes=[
                pltpu.VMEM((N, blk, R), BF16),
                pltpu.VMEM((N, blk, R), BF16),
                pltpu.VMEM((N, blk, R), BF16),
                pltpu.VMEM((2, K, T, D), BF16),
                pltpu.VMEM((2, T, D), BF16),
                pltpu.VMEM((2, T, D), BF16),
                pltpu.VMEM((2 * rows, R), F32),
                pltpu.VMEM((rows, R), BF16),
                pltpu.VMEM((2, rows, R), BF16),
                pltpu.VMEM((T, R), F32),
                pltpu.VMEM((T, R), F32),
                pltpu.VMEM((R, R), F32),
                pltpu.VMEM((K, N, T, blk), BF16),
                pltpu.VMEM((K - 1, N, T, blk), BF16),
                pltpu.VMEM((rows, R), BF16),
                pltpu.VMEM((K, T, R), F32),
                pltpu.VMEM((K, T, R), BF16),
                pltpu.VMEM((K - 1, T, R), BF16),
                pltpu.VMEM((K, 2, T, R), BF16),
                pltpu.VMEM((N, T, blk), BF16),
                pltpu.VMEM((2, N, T, blk), BF16),
                pltpu.VMEM((K - 1, N, T, blk), BF16),
                pltpu.VMEM((K - 1, N, T, blk), BF16),
                pltpu.VMEM((K - 2, N, T, blk), F32),
                pltpu.VMEM((2, H, blk, R), BF16),
                pltpu.VMEM((2, H, blk, R), BF16),
                pltpu.SMEM((N, K, S), jnp.int32),
                dma((6,)),
                dma((K - 1, N)),
                dma((2, 2, H)),
                dma((2, 2, H)),
                dma((H + 1, 2)),
                dma((H + 1, 2)),
                dma((3, 2)),
                dma((3, 2)),
                dma,
                dma,
                dma((K - 1,)),
                dma((K - 1,)),
                dma((K - 2, 3)),
                dma((K - 2, 3)),
                dma((N,)),
                dma((K, 2)),
                dma((K, 2)),
                dma((K - 1,)),
                dma((K - 1,)),
                dma((2, H, 4)),
                dma((2, H, 4)),
            ],
            compiler_params=pltpu.CompilerParams(
                collective_id=0, has_side_effects=True, vmem_limit_bytes=60 * 1024 * 1024
            ),
        )(saved, incoming, head, wd, wu, adopt.transpose(1, 2, 0), live)
        return pl.pallas_call(
            hand_over,
            out_shape=tuple(jax.ShapeDtypeStruct(r.shape, r.dtype) for r in results),
            in_specs=[vmem] * 2,
            out_specs=(vmem, vmem),
        )(*results)

    return jax.shard_map(
        body,
        mesh=mesh,
        in_specs=(
            P("section", "dp", None, None, None, None),
            P("section", "dp", None, None, None),
            P(None, "dp", None, None),
            P("section", "dp", None),
            P("section", "dp", None),
            P(),
            P(),
        ),
        out_specs=(P("section", "dp", None, None, None), P("section", "dp", None)),
        check_vma=False,
    )
```
